32 devices in a mesh: fsdp: 8 (over z, x), tp: 4 (over y, core).
Axes of the slice: x: 2, y: 2, z: 4, core: 2. Of those that a mesh axis runs over, the one named last changes fastest.
Arguments:
- layer_input_rows: bfloat16 [8, 2048, 1024], P(None, 'fsdp'), may hold values from -6 to 6
- sequence_lengths: int32 [8, 2], replicated, may hold values from 0 to 2048, as said below
- attn_gain: bfloat16 [1024], P('fsdp'), may hold values from 0.5 to 1.5
- qkv_weight: bfloat16 [1024, 3, 8, 128], P('fsdp', None, 'tp'), may hold values from -0.1875 to 0.1875
- conv_weight: bfloat16 [4, 3, 8, 128], P(None, None, 'tp', 'fsdp'), may hold values from -3 to 3
- beta_weight: bfloat16 [1024, 8], P('fsdp', 'tp'), may hold values from -0.375 to 0.375
- beta_bias: bfloat16 [8], P('tp'), may hold values from -7 to 0
- out_gain: bfloat16 [128], P('fsdp'), may hold values from 0.5 to 1.5
- out_weight: bfloat16 [8, 128, 1024], P('tp', None, 'fsdp'), may hold values from -0.1875 to 0.1875
- mlp_gain: bfloat16 [1024], P('fsdp'), may hold values from 0.5 to 1.5
- gate_up_weight: bfloat16 [1024, 2, 2816], P('fsdp', None, 'tp'), may hold values from -0.1875 to 0.1875
- down_weight: bfloat16 [2816, 1024], P('tp', 'fsdp'), may hold values from -0.109375 to 0.109375
- cotangent: bfloat16 [8, 2048, 1024], P(None, 'fsdp'), may hold values from -6 to 6
Outputs:
- layer_output: bfloat16 [8, 2048, 1024], P(None, ('fsdp', 'tp'))
- input_grad: float32 [8, 2048, 1024], P(None, ('fsdp', 'tp'))
- attn_gain_grad: float32 [1024], P('fsdp')
- qkv_grad: float32 [1024, 3, 8, 128], P('fsdp', None, 'tp')
- conv_grad: float32 [4, 3, 8, 128], P(None, None, 'tp', 'fsdp')
- beta_weight_grad: float32 [1024, 8], P('fsdp', 'tp')
- beta_bias_grad: float32 [8], P('tp')
- out_gain_grad: float32 [128], P('fsdp')
- out_weight_grad: float32 [8, 128, 1024], P('tp', None, 'fsdp')
- mlp_gain_grad: float32 [1024], P('fsdp')
- gate_up_grad: float32 [1024, 2, 2816], P('fsdp', None, 'tp')
- down_grad: float32 [2816, 1024], P('tp', 'fsdp')
The draws below stay inside these ranges and needn't reach their ends.
Inputs may be any that keep to these rules, and one draw needn't show every extreme that they name: Row r holds its sequences end to end from position 0 in the slots of sequence_lengths[r], each a multiple of 64 and 1024 or more long, followed by zeros; the row's positions past their sum are padding. One row holds a single sequence of 2048 positions and another one holds a sequence of 1024 positions in every draw.
All inputs are finite; a program needn't handle non-finite values.
Results may differ from the reference program's by a relative error of at most 0.024.
Values may be sent and summed in bfloat16 or wider, within the bound.
No kernel may reach another device: no remote copies, remote signals or barrier semaphores. Data moves between devices by JAX's collectives and lax.ppermute only.
A program may use at most 192 MiB of HBM per device.

```python
import math
import jax
import jax.numpy as jnp
from jax import lax

MODEL_WIDTH = 1024
H = 8
DK = 128
FF = 2816
CONV_TAP_COUNT = 4
DELTA_SPAN = 64
LEAST_LENGTH = 1024
PACKED_ROWS = 8
ROW_LENGTH = 2048


def draw_sequence_lengths(key, part):
    key = jax.random.fold_in(key, 11)
    random_keys = jax.random.split(key, 7)
    segment_count = ROW_LENGTH // LEAST_LENGTH
    iteration_count = LEAST_LENGTH // DELTA_SPAN
    order = jax.random.permutation(random_keys[4], PACKED_ROWS)
    short_row = order == 1
    level = jnp.minimum(jax.random.randint(random_keys[0], (PACKED_ROWS, segment_count), 0, 4), jax.random.randint(random_keys[1], (PACKED_ROWS, segment_count), 0, 4))
    growth_scale = jnp.left_shift(jnp.ones_like(level), level)
    desired_length = jnp.minimum(LEAST_LENGTH * growth_scale + DELTA_SPAN * jax.random.randint(random_keys[2], (PACKED_ROWS, segment_count), 0, iteration_count), ROW_LENGTH)
    padding_amount = DELTA_SPAN * jax.random.randint(random_keys[3], (PACKED_ROWS,), 0, ROW_LENGTH // (32 * DELTA_SPAN) + 2)
    padding_amount = jnp.where(short_row, 0, padding_amount)
    remaining_space = ROW_LENGTH - padding_amount - jnp.where(short_row, LEAST_LENGTH, 0)
    first_cap = LEAST_LENGTH + DELTA_SPAN * jax.random.randint(random_keys[5], (PACKED_ROWS,), 0, (remaining_space - LEAST_LENGTH) // DELTA_SPAN + 1)
    first_cap = jnp.where(short_row, first_cap, remaining_space)
    desired_length = desired_length.at[:, 0].set(jnp.minimum(desired_length[:, 0], first_cap))
    ends = jnp.cumsum(desired_length, 1)
    taken = ends <= remaining_space[:, None]
    kept = jnp.where(taken, desired_length, 0)
    count = jnp.sum(taken.astype(jnp.int32), 1)
    left = remaining_space - jnp.sum(kept, 1)
    segment_index = jnp.arange(segment_count)
    fresh = (left >= LEAST_LENGTH) & (count < segment_count)
    kept = kept + jnp.where(fresh[:, None] & (segment_index[None, :] == count[:, None]), left[:, None], 0)
    kept = kept + jnp.where(jnp.logical_not(fresh)[:, None] & (segment_index[None, :] == count[:, None] - 1), left[:, None], 0)
    total_count = count + fresh.astype(jnp.int32)
    insert_at = jax.random.randint(random_keys[6], (PACKED_ROWS,), 0, total_count + 1)
    shifted = jnp.concatenate([jnp.zeros((PACKED_ROWS, 1), kept.dtype), kept[:, :segment_count - 1]], 1)
    placed = jnp.where(segment_index[None, :] < insert_at[:, None], kept, jnp.where(segment_index[None, :] == insert_at[:, None], LEAST_LENGTH, shifted))
    kept = jnp.where(short_row[:, None], placed, kept)
    complete_row = jnp.where(segment_index == 0, ROW_LENGTH, 0)
    kept = jnp.where((order == 0)[:, None], complete_row[None, :], kept)
    return kept.astype(jnp.int32)


def shard_levels(key, extent, shards, smallest, high):
    gain = 1.0
    for axis_at, parts in shards:
        draws = jax.random.uniform(jax.random.fold_in(jax.random.fold_in(key, 6), axis_at), (parts,), jnp.float32, smallest / len(shards), high / len(shards))
        gain = gain * jnp.repeat(jnp.exp(draws), extent[axis_at] // parts).reshape((-1,) + (1,) * (len(extent) - 1 - axis_at))
    return gain


def bell_draw(rng, shape, deviation, bound, pieces=(), kind=jnp.bfloat16):
    level = shard_levels(rng, shape, pieces, -0.22, 0.18) if pieces else 1.0
    values = jax.random.normal(rng, shape, jnp.float32) * deviation * level
    return jnp.minimum(jnp.maximum(values, -bound), bound).astype(kind)


def setup_inputs(seed: int = 0) -> dict:
    key_list = jax.random.split(jax.random.key(seed), 14)
    layer_input_rows = bell_draw(key_list[0], (PACKED_ROWS, ROW_LENGTH, MODEL_WIDTH), 1.0, 6.0, ((1, 8),))
    sequence_lengths = draw_sequence_lengths(jax.random.fold_in(key_list[13], 71), 0)
    attn_gain = jnp.clip(1.0 + 0.1 * jax.random.normal(key_list[2], (MODEL_WIDTH,), jnp.float32), 0.5, 1.5).astype(jnp.bfloat16)
    qkv_weight = bell_draw(key_list[3], (MODEL_WIDTH, 3, H, DK), MODEL_WIDTH ** -0.5, 0.1875, ((0, 8), (2, 4)))
    conv_weight = bell_draw(key_list[4], (CONV_TAP_COUNT, 3, H, DK), 0.5, 3.0, ((2, 4), (3, 8)))
    beta_weight = bell_draw(key_list[5], (MODEL_WIDTH, H), (MODEL_WIDTH // 4) ** -0.5, 0.375, ((0, 8), (1, 4)))
    beta_bias = jnp.clip(-7.0 + 7.0 * jax.random.uniform(key_list[6], (H,), jnp.float32) ** shard_levels(key_list[6], (H,), ((0, 4),), -0.2, 0.2), -7.0, 0.0).astype(jnp.bfloat16)
    out_gain = jnp.clip(1.0 + 0.1 * jax.random.normal(key_list[7], (DK,), jnp.float32), 0.5, 1.5).astype(jnp.bfloat16)
    out_weight = bell_draw(key_list[8], (H, DK, MODEL_WIDTH), (H * DK) ** -0.5, 0.1875, ((0, 4), (2, 8)))
    mlp_gain = jnp.clip(1.0 + 0.1 * jax.random.normal(key_list[9], (MODEL_WIDTH,), jnp.float32), 0.5, 1.5).astype(jnp.bfloat16)
    gate_up_weight = bell_draw(key_list[10], (MODEL_WIDTH, 2, FF), MODEL_WIDTH ** -0.5, 0.1875, ((0, 8), (2, 4)))
    down_weight = bell_draw(key_list[11], (FF, MODEL_WIDTH), FF ** -0.5, 0.109375, ((0, 4), (1, 8)))
    cotangent = bell_draw(key_list[12], (PACKED_ROWS, ROW_LENGTH, MODEL_WIDTH), 1.0, 6.0, ((1, 8),))
    return {"layer_input_rows": layer_input_rows, "sequence_lengths": sequence_lengths, "attn_gain": attn_gain, "qkv_weight": qkv_weight, "conv_weight": conv_weight, "beta_weight": beta_weight, "beta_bias": beta_bias, "out_gain": out_gain, "out_weight": out_weight, "mlp_gain": mlp_gain, "gate_up_weight": gate_up_weight, "down_weight": down_weight, "cotangent": cotangent}


EPS_NORM = 1e-05
EPS_UNIT = 1e-06
HIGH = lax.Precision.HIGHEST

@jax.custom_vjp
def low(v):
    return lax.optimization_barrier(v.astype(jnp.bfloat16)).astype(jnp.float32)

@jax.custom_vjp
def low_back(v):
    return v

def low_keep(v):
    return (low(v), None)

def low_pass(kept, grad):
    return (grad,)

def back_keep(v):
    return (v, None)

def back_low(kept, grad):
    return (low(grad),)
low.defvjp(low_keep, low_pass)
low_back.defvjp(back_keep, back_low)

def product(left_mat, right_mat):
    return jnp.einsum('...ij,...jk->...ik', left_mat, right_mat, precision=HIGH)

def packing_layout(sequence_lengths, first_pos, seg_len, tap_count):
    ends = jnp.cumsum(sequence_lengths, 1).astype(jnp.int32)
    starts = ends - sequence_lengths
    ext_pos = first_pos - (tap_count - 1) + jnp.arange(seg_len + tap_count - 1, dtype=jnp.int32)
    doc_ext = lax.optimization_barrier(jnp.sum((ext_pos[None, :, None] >= ends[:, None, :]).astype(jnp.int32), -1))
    own_pos = ext_pos[tap_count - 1:]
    own_doc = doc_ext[:, tap_count - 1:]
    padding_mask = (own_pos[None, :] < ends[:, -1:]).astype(jnp.float32)
    taps = []
    for tap_index in range(tap_count):
        offset = tap_count - 1 - tap_index
        same = (doc_ext[:, offset:offset + seg_len] == own_doc) & (ext_pos[None, offset:offset + seg_len] >= 0)
        taps.append(same.astype(jnp.float32))
    convolution_mask = jnp.stack(taps, -1)
    block_pos = first_pos + DELTA_SPAN * jnp.arange(seg_len // DELTA_SPAN, dtype=jnp.int32)
    begins = jnp.any((block_pos[None, :, None] == starts[:, None, :]) & (sequence_lengths[:, None, :] > 0), -1)
    retained_blocks = jnp.transpose(1.0 - begins.astype(jnp.float32))
    return (padding_mask, convolution_mask, retained_blocks)

def wy_form(key_rows, value_rows, rate_rows):
    block_len = key_rows.shape[-2]
    gram_mat = jnp.einsum('...ik,...jk->...ij', key_rows, key_rows, precision=HIGH)
    lower_mask = jnp.tril(jnp.ones((block_len, block_len), jnp.float32), -1)
    system = jnp.eye(block_len, dtype=jnp.float32) + lower_mask * rate_rows[..., :, None] * gram_mat
    weighted_keys = jax.scipy.linalg.solve_triangular(system, rate_rows[..., None] * key_rows, lower=True, unit_diagonal=True)
    weighted_vals = jax.scipy.linalg.solve_triangular(system, rate_rows[..., None] * value_rows, lower=True, unit_diagonal=True)
    return (weighted_keys, weighted_vals)

def group_step(state_mat, block_in):
    query_rows, key_rows, value_rows, rate_rows, keep_rows = block_in
    state_mat = state_mat * keep_rows[:, None, None, None]
    weighted_keys, weighted_vals = wy_form(key_rows, value_rows, rate_rows)
    fresh_vals = weighted_vals - product(weighted_keys, state_mat)
    block_len = key_rows.shape[-2]
    causal = jnp.tril(jnp.ones((block_len, block_len), jnp.float32))
    scores = causal * jnp.einsum('...ik,...jk->...ij', query_rows, key_rows, precision=HIGH)
    outputs = product(query_rows, state_mat) + product(scores, fresh_vals)
    key_cols = jnp.swapaxes(key_rows, -1, -2)
    return (state_mat + product(key_cols, fresh_vals), outputs)

def to_blocks(values):
    shape = values.shape
    return values.reshape(shape[0], shape[1] // DELTA_SPAN, DELTA_SPAN, shape[2], shape[3]).transpose(1, 0, 3, 2, 4)

def rate_blocks(values):
    shape = values.shape
    return values.reshape(shape[0], shape[1] // DELTA_SPAN, DELTA_SPAN, shape[2]).transpose(1, 0, 3, 2)

def from_blocks(blocks):
    shape = blocks.shape
    return blocks.transpose(1, 0, 3, 2, 4).reshape(shape[1], shape[0] * shape[3], shape[2], shape[4])

def unit_rows(values):
    return values / jnp.sqrt(lax.optimization_barrier(jnp.sum(values * values, -1, keepdims=True)) + EPS_UNIT)

def rms_unit(values):
    return values * lax.rsqrt(lax.optimization_barrier(jnp.mean(values * values, -1, keepdims=True)) + EPS_NORM)

def features(extended, rate_logit, conv_taps, convolution_mask, padding_mask):
    tap_count = conv_taps.shape[0]
    seg_len = rate_logit.shape[1]
    conv_out = jnp.zeros_like(extended[:, :seg_len])
    for tap_index in range(tap_count):
        offset = tap_count - 1 - tap_index
        conv_out = conv_out + conv_taps[tap_index] * extended[:, offset:offset + seg_len] * convolution_mask[:, :, tap_index, None, None, None]
    active = jax.nn.silu(conv_out)
    queries = unit_rows(active[:, :, 0]) / math.sqrt(active.shape[-1])
    key_vecs = unit_rows(active[:, :, 1])
    value_vecs = active[:, :, 2]
    rates_all = jax.nn.sigmoid(rate_logit) * padding_mask[..., None]
    return (queries, key_vecs, value_vecs, rates_all)

def delta_rule(queries, key_vecs, value_vecs, rates_all, retained_blocks, state_start):
    blocks_in = (to_blocks(queries), to_blocks(key_vecs), to_blocks(value_vecs), rate_blocks(rates_all), retained_blocks)
    final_state, outputs = lax.scan(jax.checkpoint(group_step), state_start, blocks_in)
    return (from_blocks(outputs), final_state)

def forward(layer_input_rows, attn_gain, qkv_weight, conv_weight, beta_weight, beta_bias, out_gain, out_weight, mlp_gain, gate_up_weight, down_weight, padding_mask, convolution_mask, retained_blocks):
    normed_in = low(rms_unit(layer_input_rows) * attn_gain)
    projected = low_back(jnp.einsum('rtd,dchk->rtchk', normed_in, qkv_weight, precision=HIGH))
    rate_logit = low_back(jnp.einsum('rtd,dh->rth', normed_in, beta_weight, precision=HIGH)) + beta_bias
    extended = jnp.pad(projected, ((0, 0), (CONV_TAP_COUNT - 1, 0), (0, 0), (0, 0), (0, 0)))
    queries, key_vecs, value_vecs, rates_all = features(extended, rate_logit, conv_weight, convolution_mask, padding_mask)
    state_start = jnp.zeros((PACKED_ROWS, H, DK, DK), jnp.float32)
    mixed, final_state = delta_rule(queries, key_vecs, value_vecs, rates_all, retained_blocks, state_start)
    mixed_low = low(rms_unit(mixed) * out_gain * padding_mask[..., None, None])
    residual = layer_input_rows + low_back(jnp.einsum('rthk,hkd->rtd', mixed_low, out_weight, precision=HIGH))
    normed_mid = low(rms_unit(residual) * mlp_gain)
    gate_up = low_back(jnp.einsum('rtd,dcf->rtcf', normed_mid, gate_up_weight, precision=HIGH))
    hidden = low(jax.nn.silu(gate_up[:, :, 0]) * gate_up[:, :, 1])
    return residual + jnp.einsum('rtf,fd->rtd', hidden, down_weight, precision=HIGH)

def reference(layer_input_rows, sequence_lengths, attn_gain, qkv_weight, conv_weight, beta_weight, beta_bias, out_gain, out_weight, mlp_gain, gate_up_weight, down_weight, cotangent):
    padding_mask, convolution_mask, retained_blocks = packing_layout(sequence_lengths, 0, ROW_LENGTH, CONV_TAP_COUNT)
    params = (layer_input_rows, attn_gain, qkv_weight, conv_weight, beta_weight, beta_bias, out_gain, out_weight, mlp_gain, gate_up_weight, down_weight)
    params = tuple((item.astype(jnp.float32) for item in params))

    def layer_fn(*inputs):
        return forward(*inputs, padding_mask, convolution_mask, retained_blocks)
    result, pullback = jax.vjp(layer_fn, *params)
    grads = pullback(cotangent.astype(jnp.float32))
    return (result.astype(jnp.bfloat16), grads[0], grads[1], grads[2], grads[3], grads[4], grads[5], grads[6], grads[7], grads[8], grads[9], grads[10])
```

```python
import math

import jax
import jax.numpy as jnp
from jax import lax
from jax.experimental import pallas as pl
from jax.experimental.pallas import tpu as pltpu
from jax.sharding import PartitionSpec as P

BF = jnp.bfloat16
F32 = jnp.float32
EPS_NORM = 1e-05
EPS_UNIT = 1e-06
RIM = 16
LANES = 128
VMEM_BYTES = 44 << 20


def dot(left, right):
    return lax.dot_general(left, right, (((1,), (0,)), ((), ())), preferred_element_type=F32)


def dot_nt(left, right):
    return lax.dot_general(left, right, (((1,), (1,)), ((), ())), preferred_element_type=F32)


def dot_tn(left, right):
    return lax.dot_general(left, right, (((0,), (0,)), ((), ())), preferred_element_type=F32)


def split(value):
    high = value.astype(BF)
    return high, (value - high.astype(F32)).astype(BF)


def left_pair(high, low):
    return jnp.concatenate([high, low], 1)


def right_pair(high, low):
    top = jnp.concatenate([high, low], 1)
    bottom = jnp.concatenate([high, jnp.zeros_like(low)], 1)
    return jnp.concatenate([top, bottom], 0)


def fold(both):
    half = both.shape[1] // 2
    return both[:, :half] + both[:, half:]


def doc_at(position, ends_ref, row):
    total = jnp.zeros_like(position)
    for slot in range(ends_ref.shape[1]):
        total = total + (position >= ends_ref[row, slot]).astype(jnp.int32)
    return total


def row_masks(ends_ref, first_ref, row, seg_len):
    first = first_ref[0]
    pos_cols = first + lax.broadcasted_iota(jnp.int32, (seg_len, LANES), 0)
    pos_rows = first + lax.broadcasted_iota(jnp.int32, (1, seg_len), 1)
    doc_cols = doc_at(pos_cols, ends_ref, row)
    doc_rows = doc_at(pos_rows, ends_ref, row)
    doc_before = doc_at(first - 1, ends_ref, row)
    doc_last = doc_at(first + seg_len - 1, ends_ref, row)
    entering = (doc_cols == doc_before).astype(F32)
    leaving = (doc_cols == doc_last).astype(F32)
    whole = (doc_before == doc_last).astype(F32)
    pad = (pos_cols < ends_ref[row, ends_ref.shape[1] - 1]).astype(F32)
    same = doc_cols[:, :1] == doc_rows
    return pos_cols, doc_cols, entering, leaving, whole, pad, same


def tap_masks(pos_cols, doc_cols, ends_ref, row, tap_count):
    return [None] + [
        (doc_at(pos_cols - tap, ends_ref, row) == doc_cols).astype(F32)
        for tap in range(1, tap_count)
    ]


def conv_tile(ext_ref, taps, tap_ref, lane, seg_len):
    cols = pl.ds(lane, LANES)
    total = tap_ref[0:1, cols] * ext_ref[pl.ds(RIM, seg_len), cols]
    for tap in range(1, len(taps)):
        total = total + tap_ref[tap : tap + 1, cols] * (
            ext_ref[pl.ds(RIM - tap, seg_len), cols] * taps[tap]
        )
    return total


def sigmoid(value):
    return 1.0 / (1.0 + jnp.exp(-value))


def triangle_inverse(lower):
    size = lower.shape[0]
    if size > LANES:
        half = size // 2
        top = triangle_inverse(lower[:half, :half])
        end = triangle_inverse(lower[half:, half:])
        cross = product3(product3(end, lower[half:, :half]), top)
        upper = jnp.concatenate([top, jnp.zeros((half, half), F32)], 1)
        return jnp.concatenate([upper, jnp.concatenate([-cross, end], 1)], 0)
    at_row = lax.broadcasted_iota(jnp.int32, (size, size), 0)
    at_col = lax.broadcasted_iota(jnp.int32, (size, size), 1)
    eye = (at_row == at_col).astype(F32)
    inverse = eye - jnp.where((at_row ^ at_col) == 1, lower, 0.0)
    step = 1
    while (2 << step) <= size:
        level = jnp.where(((at_row >> step) ^ (at_col >> step)) == 1, lower, 0.0)
        high, low = split(inverse)
        across = fold(dot(left_pair(high, low), right_pair(*split(level))))
        inverse = inverse - fold(dot(left_pair(*split(across)), right_pair(high, low)))
        step += 1
    return inverse


def product3(left, right):
    return fold(dot(left_pair(*split(left)), right_pair(*split(right))))


def mix_kernel(
    ends_ref, first_ref, bias_ref, x_ref, rim_ref, gain_ref, w_ref, tap_ref,
    normed_ref, ext_out_ref, query_ref, local_ref, inv_ref, decay_ref, state_ref,
    ext_ref,
):
    row = pl.program_id(0)
    seg_len = x_ref.shape[1]
    heads = inv_ref.shape[1]
    width = tap_ref.shape[1]
    whole_x = jnp.concatenate([rim_ref[0], x_ref[0]], 0).astype(F32)
    scale = lax.rsqrt(jnp.mean(whole_x * whole_x, -1, keepdims=True) + EPS_NORM)
    normed = (whole_x * scale * gain_ref[...]).astype(BF)
    normed_ref[0] = normed[RIM:]
    ext_ref[...] = dot(normed, w_ref[...])
    ext_out_ref[0] = ext_ref[...]
    pos_cols, doc_cols, entering, leaving, whole, pad, same = row_masks(
        ends_ref, first_ref, row, seg_len
    )
    taps = tap_masks(pos_cols, doc_cols, ends_ref, row, tap_ref.shape[0])
    at_row = lax.broadcasted_iota(jnp.int32, (seg_len, seg_len), 0)
    at_col = lax.broadcasted_iota(jnp.int32, (seg_len, seg_len), 1)
    strict = same & (at_row > at_col)
    causal = same & (at_row >= at_col)
    eye = (
        lax.broadcasted_iota(jnp.int32, (LANES, LANES), 0)
        == lax.broadcasted_iota(jnp.int32, (LANES, LANES), 1)
    ).astype(F32)
    for head in range(heads):
        active = []
        for part in range(3):
            conv = conv_tile(ext_ref, taps, tap_ref, (part * heads + head) * LANES, seg_len)
            active.append(conv * sigmoid(conv))
        query, key, value = active
        query = query * (
            lax.rsqrt(jnp.sum(query * query, -1, keepdims=True) + EPS_UNIT)
            * (1.0 / math.sqrt(LANES))
        )
        key = key * lax.rsqrt(jnp.sum(key * key, -1, keepdims=True) + EPS_UNIT)
        logit = ext_ref[pl.ds(RIM, seg_len), pl.ds(width, LANES)][:, head : head + 1]
        rate = sigmoid(logit + bias_ref[head]) * pad[:, :1]
        key_low = key.astype(BF)
        gram = dot_nt(key_low, key_low)
        lower = jnp.where(strict, rate * gram, 0.0)
        inverse = triangle_inverse(lower).astype(BF)
        inv_ref[0, head] = inverse
        right = jnp.concatenate([rate * entering * key, rate * value], 1).astype(BF)
        weighted = dot(inverse, right).astype(BF)
        scores = jnp.where(causal, dot_nt(query.astype(BF), key_low), 0.0).astype(BF)
        mixed = dot(scores, weighted)
        lanes = pl.ds(head * LANES, LANES)
        query_ref[0, :, lanes] = (entering * query - mixed[:, :LANES]).astype(BF)
        local_ref[0, :, lanes] = mixed[:, LANES:]
        ends_state = dot_tn((leaving * key).astype(BF), weighted)
        decay_ref[0, head] = whole * eye - ends_state[:, :LANES]
        state_ref[0, head] = ends_state[:, LANES:]


def head_kernel(
    ends_ref, first_ref, query_ref, local_ref, state_ref, gain_ref, out_ref,
    mixed_ref, low_ref, attn_ref,
):
    row = pl.program_id(0)
    seg_len = query_ref.shape[1]
    heads = state_ref.shape[1]
    pos = first_ref[0] + lax.broadcasted_iota(jnp.int32, (seg_len, LANES), 0)
    pad = (pos < ends_ref[row, ends_ref.shape[1] - 1]).astype(F32)
    for head in range(heads):
        lanes = pl.ds(head * LANES, LANES)
        mixed = local_ref[0, :, lanes] + dot(query_ref[0, :, lanes], state_ref[0, head])
        mixed_ref[0, :, lanes] = mixed
        scale = lax.rsqrt(jnp.mean(mixed * mixed, -1, keepdims=True) + EPS_NORM)
        low_ref[0, :, lanes] = (mixed * scale * gain_ref[...] * pad).astype(BF)
    attn_ref[0] = dot(low_ref[0], out_ref[...]).astype(BF)


def head_back_kernel(
    ends_ref, first_ref, grad_ref, out_ref, gain_ref, mixed_ref, query_ref,
    grad_mixed_ref, state_ref, gain_grad_ref,
):
    row = pl.program_id(0)
    seg_len = query_ref.shape[1]
    heads = state_ref.shape[1]
    pos = first_ref[0] + lax.broadcasted_iota(jnp.int32, (seg_len, LANES), 0)
    pad = (pos < ends_ref[row, ends_ref.shape[1] - 1]).astype(F32)

    @pl.when(row == 0)
    def _():
        gain_grad_ref[...] = jnp.zeros_like(gain_grad_ref)

    grads = dot_nt(grad_ref[0], out_ref[...])
    for head in range(heads):
        lanes = pl.ds(head * LANES, LANES)
        mixed = mixed_ref[0, :, lanes]
        scale = lax.rsqrt(jnp.mean(mixed * mixed, -1, keepdims=True) + EPS_NORM)
        unit = mixed * scale
        grad = grads[:, head * LANES : (head + 1) * LANES] * pad
        gain_grad_ref[0:1, :] += jnp.sum(grad * unit, 0, keepdims=True)
        grad = grad * gain_ref[...]
        grad = scale * (grad - unit * jnp.mean(grad * unit, -1, keepdims=True))
        low = grad.astype(BF)
        grad_mixed_ref[0, :, lanes] = low
        state_ref[0, head] = dot_tn(query_ref[0, :, lanes], low)


def mix_back_kernel(
    ends_ref, first_ref, bias_ref, ext_ref, tap_ref, inv_ref, grad_ref, state_ref, leave_ref,
    proj_ref, tail_ref, rim_ref, tap_grad_ref, bias_grad_ref,
    conv_ref,
):
    row = pl.program_id(0)
    seg_len = grad_ref.shape[1]
    heads = inv_ref.shape[1]
    width = tap_ref.shape[1]
    tap_count = tap_ref.shape[0]

    @pl.when(row == 0)
    def _():
        tap_grad_ref[...] = jnp.zeros_like(tap_grad_ref)
        bias_grad_ref[...] = jnp.zeros_like(bias_grad_ref)

    conv_ref[pl.ds(0, RIM), :] = jnp.zeros((RIM, width), F32)
    conv_ref[pl.ds(RIM + seg_len, RIM), :] = jnp.zeros((RIM, width), F32)
    ext = ext_ref.at[0]
    pos_cols, doc_cols, entering, leaving, whole, pad, same = row_masks(
        ends_ref, first_ref, row, seg_len
    )
    taps = tap_masks(pos_cols, doc_cols, ends_ref, row, tap_count)
    at_row = lax.broadcasted_iota(jnp.int32, (seg_len, seg_len), 0)
    at_col = lax.broadcasted_iota(jnp.int32, (seg_len, seg_len), 1)
    strict = same & (at_row > at_col)
    causal = same & (at_row >= at_col)
    lane_at = lax.broadcasted_iota(jnp.int32, (seg_len, LANES), 1)
    logit_grads = jnp.zeros((seg_len, LANES), F32)
    for head in range(heads):
        convs, gates, active = [], [], []
        for part in range(3):
            conv = conv_tile(ext, taps, tap_ref, (part * heads + head) * LANES, seg_len)
            gate = sigmoid(conv)
            convs.append(conv)
            gates.append(gate)
            active.append(conv * gate)
        query_size = lax.rsqrt(jnp.sum(active[0] * active[0], -1, keepdims=True) + EPS_UNIT)
        key_size = lax.rsqrt(jnp.sum(active[1] * active[1], -1, keepdims=True) + EPS_UNIT)
        query_unit = active[0] * query_size
        key = active[1] * key_size
        value = active[2]
        logit = ext[pl.ds(RIM, seg_len), pl.ds(width, LANES)][:, head : head + 1]
        gate_rate = sigmoid(logit + bias_ref[head])
        rate = gate_rate * pad[:, :1]
        query_low = (query_unit * (1.0 / math.sqrt(LANES))).astype(BF)
        key_low = key.astype(BF)
        state = state_ref[0, head]
        leave = leave_ref[0, head]
        inverse = inv_ref[0, head]
        lanes = pl.ds(head * LANES, LANES)
        grad = grad_ref[0, :, lanes]
        missing = value - entering * dot(key_low, state)
        fresh = dot(inverse, (rate * missing).astype(BF)).astype(BF)
        scores = jnp.where(causal, dot_nt(query_low, key_low), 0.0).astype(BF)
        leaving_key = (leaving * key).astype(BF)
        fresh_grad = dot_tn(scores, grad) + dot(leaving_key, leave)
        solved = dot_tn(inverse, fresh_grad.astype(BF))
        solved_low = solved.astype(BF)
        score_grad = jnp.where(causal, dot_nt(grad, fresh), 0.0).astype(BF)
        lower_grad = jnp.where(strict, -dot_nt(solved_low, fresh), 0.0)
        lower_low = lower_grad.astype(BF)
        rate_low = (rate * lower_grad).astype(BF)
        query_grad = entering * dot_nt(grad, state) + dot(score_grad, key_low)
        lower_key = dot(lower_low, key_low)
        value_grad = rate * solved
        key_grad = (
            dot_tn(score_grad, query_low)
            + leaving * dot_nt(fresh, leave)
            - entering * dot_nt(value_grad.astype(BF), state)
            + rate * lower_key
            + dot_tn(rate_low, key_low)
        )
        rate_grad = jnp.sum(solved * missing + key * lower_key, -1, keepdims=True)
        logit_grad = rate_grad * rate * (1.0 - gate_rate)
        logit_grads = logit_grads + jnp.where(lane_at == head, logit_grad, 0.0)
        query_grad = query_grad * (1.0 / math.sqrt(LANES))
        query_grad = query_size * (
            query_grad - query_unit * jnp.sum(query_unit * query_grad, -1, keepdims=True)
        )
        key_grad = key_size * (key_grad - key * jnp.sum(key * key_grad, -1, keepdims=True))
        for part, active_grad in enumerate((query_grad, key_grad, value_grad)):
            conv_grad = active_grad * (gates[part] * (1.0 + convs[part] * (1.0 - gates[part])))
            lane = (part * heads + head) * LANES
            cols = pl.ds(lane, LANES)
            conv_ref[pl.ds(RIM, seg_len), cols] = conv_grad
            for tap in range(tap_count):
                masked = conv_grad if tap == 0 else conv_grad * taps[tap]
                tap_grad_ref[tap : tap + 1, cols] += jnp.sum(
                    masked * ext[pl.ds(RIM - tap, seg_len), cols], 0, keepdims=True
                )
    bias_grad_ref[0:1, :] += jnp.sum(logit_grads, 0, keepdims=True)
    first = first_ref[0] - RIM
    pos_ext = first + lax.broadcasted_iota(jnp.int32, (seg_len + RIM, LANES), 0)
    doc_ext = doc_at(pos_ext, ends_ref, row)
    back_masks = [None] + [
        (doc_at(pos_ext + tap, ends_ref, row) == doc_ext).astype(F32) for tap in range(1, tap_count)
    ]
    for lane in range(0, width, LANES):
        cols = pl.ds(lane, LANES)
        total = tap_ref[0:1, cols] * conv_ref[pl.ds(0, seg_len + RIM), cols]
        for tap in range(1, tap_count):
            total = total + tap_ref[tap : tap + 1, cols] * (
                conv_ref[pl.ds(tap, seg_len + RIM), cols] * back_masks[tap]
            )
        rim_ref[0, :, cols] = total[:RIM].astype(BF)
        tail_ref[0, :, cols] = total[seg_len:]
        proj_ref[0, :, cols] = total[RIM:].astype(BF)
    proj_ref[0, :, pl.ds(width, LANES)] = logit_grads.astype(BF)


def smem():
    return pl.BlockSpec(memory_space=pltpu.SMEM)


def per_row(shape):
    return pl.BlockSpec((1,) + shape, lambda row: (row,) + (0,) * len(shape))


def fixed(shape):
    return pl.BlockSpec(shape, lambda row: (0,) * len(shape))


def params():
    return pltpu.CompilerParams(
        dimension_semantics=("arbitrary",), vmem_limit_bytes=VMEM_BYTES
    )


def shaped(shape, kind):
    return jax.ShapeDtypeStruct(shape, kind)


def mix_forward(ends, first, bias, rows, rim, gain, weight, taps, heads):
    count, seg_len, model = rows.shape
    wide = weight.shape[1]
    both = heads * LANES
    return pl.pallas_call(
        mix_kernel,
        grid=(count,),
        in_specs=[
            smem(), smem(), smem(), per_row((seg_len, model)), per_row((RIM, model)),
            fixed((1, model)), fixed(weight.shape), fixed(taps.shape),
        ],
        out_specs=[
            per_row((seg_len, model)), per_row((seg_len + RIM, wide)), per_row((seg_len, both)),
            per_row((seg_len, both)), per_row((heads, seg_len, seg_len)),
            per_row((heads, LANES, LANES)), per_row((heads, LANES, LANES)),
        ],
        out_shape=[
            shaped((count, seg_len, model), BF),
            shaped((count, seg_len + RIM, wide), F32),
            shaped((count, seg_len, both), BF),
            shaped((count, seg_len, both), F32),
            shaped((count, heads, seg_len, seg_len), BF),
            shaped((count, heads, LANES, LANES), F32),
            shaped((count, heads, LANES, LANES), F32),
        ],
        scratch_shapes=[pltpu.VMEM((seg_len + RIM, wide), F32)],
        compiler_params=params(),
        name="mix_forward",
    )(ends, first, bias, rows, rim, gain, weight, taps)


def head_forward(ends, first, query, local, state, gain, out_full):
    count, seg_len, both = query.shape
    model = out_full.shape[1]
    return pl.pallas_call(
        head_kernel,
        grid=(count,),
        in_specs=[
            smem(), smem(), per_row((seg_len, both)), per_row((seg_len, both)),
            per_row(state.shape[1:]), fixed((1, LANES)), fixed(out_full.shape),
        ],
        out_specs=[
            per_row((seg_len, both)), per_row((seg_len, both)), per_row((seg_len, model)),
        ],
        out_shape=[
            shaped((count, seg_len, both), F32),
            shaped((count, seg_len, both), BF),
            shaped((count, seg_len, model), BF),
        ],
        compiler_params=params(),
        name="head_forward",
    )(ends, first, query, local, state, gain, out_full)


def head_backward(ends, first, grad, out_full, gain, mixed, query, heads):
    count, seg_len, both = query.shape
    model = out_full.shape[1]
    return pl.pallas_call(
        head_back_kernel,
        grid=(count,),
        in_specs=[
            smem(), smem(), per_row((seg_len, model)), fixed(out_full.shape), fixed((1, LANES)),
            per_row((seg_len, both)), per_row((seg_len, both)),
        ],
        out_specs=[
            per_row((seg_len, both)), per_row((heads, LANES, LANES)), fixed((8, LANES)),
        ],
        out_shape=[
            shaped((count, seg_len, both), BF),
            shaped((count, heads, LANES, LANES), F32),
            shaped((8, LANES), F32),
        ],
        compiler_params=params(),
        name="head_backward",
    )(ends, first, grad, out_full, gain, mixed, query)


def mix_backward(ends, first, bias, ext, taps, inverse, grad, state, leave):
    count, seg_len, both = grad.shape
    wide = ext.shape[2]
    tap_count, width = taps.shape
    return pl.pallas_call(
        mix_back_kernel,
        grid=(count,),
        in_specs=[
            smem(), smem(), smem(), per_row(ext.shape[1:]), fixed(taps.shape),
            per_row(inverse.shape[1:]), per_row((seg_len, both)), per_row(state.shape[1:]),
            per_row(leave.shape[1:]),
        ],
        out_specs=[
            per_row((seg_len, wide)), per_row((RIM, width)), per_row((RIM, width)),
            fixed((8, width)), fixed((8, LANES)),
        ],
        out_shape=[
            shaped((count, seg_len, wide), BF),
            shaped((count, RIM, width), F32),
            shaped((count, RIM, width), BF),
            shaped((8, width), F32),
            shaped((8, LANES), F32),
        ],
        scratch_shapes=[pltpu.VMEM((seg_len + 2 * RIM, width), F32)],
        compiler_params=params(),
        name="mix_backward",
    )(ends, first, bias, ext, taps, inverse, grad, state, leave)


def shifted(value, distance):
    devices = range(lax.axis_size("fsdp"))
    route = [(i - distance, i) for i in devices if i - distance in devices]
    return lax.ppermute(value, "fsdp", route)


def swapped(value, axis, bit):
    return lax.ppermute(value, axis, [(i, i ^ bit) for i in range(lax.axis_size(axis))])


def pick(value, index, axis):
    return lax.dynamic_index_in_dim(value, index, axis, keepdims=False)


def tp_scatter(parts):
    count, seg_len, model = parts.shape
    place = lax.axis_index("tp")
    near, far = place % 2, place // 2
    slots = parts.reshape(count, 2, 2, seg_len // 4, model)
    got = swapped(pick(slots, 1 - near, 2), "tp", 1)
    sums = pick(slots, near, 2).astype(F32) + got.astype(F32)
    got = swapped(pick(sums, 1 - far, 1).astype(BF), "tp", 2)
    return pick(sums, far, 1) + got.astype(F32)


def tp_gather(own):
    count, share, model = own.shape
    place = lax.axis_index("tp")
    near, far = place % 2, place // 2
    other = swapped(own, "tp", 2)
    column = jnp.stack([jnp.where(far == 0, own, other), jnp.where(far == 0, other, own)], 1)
    other = swapped(column, "tp", 1)
    both = jnp.stack([jnp.where(near == 0, column, other), jnp.where(near == 0, other, column)], 2)
    return both.reshape(count, 4 * share, model)


def apply(maps, states):
    return jnp.einsum("rhij,rhjk->rhik", maps, states, preferred_element_type=F32)


def apply_back(maps, states):
    return jnp.einsum("rhji,rhjk->rhik", maps, states, preferred_element_type=F32)


def halves(value, place):
    count = value.shape[0] // 2
    pair = value.reshape((2, count) + value.shape[1:])
    return pick(pair, place, 0), pick(pair, 1 - place, 0)


def joined(kept, got, place):
    first = jnp.where(place == 0, kept, got)
    second = jnp.where(place == 0, got, kept)
    return jnp.concatenate([first, second], 0)


def relay_forward(decay, local):
    place = lax.axis_index("fsdp") % 2
    turns = lax.axis_size("fsdp") // 2 - 1
    decay, local = decay.astype(BF), local.astype(BF)
    own_decay, send_decay = halves(decay, place)
    own_local, send_local = halves(local, place)
    got_decay, got_local = swapped((send_decay, send_local), "fsdp", 1)
    first_decay = jnp.where(place == 0, own_decay, got_decay)
    first_local = jnp.where(place == 0, own_local, got_local)
    second_decay = jnp.where(place == 0, got_decay, own_decay)
    second_local = jnp.where(place == 0, got_local, own_local)
    pair_decay = apply(second_decay, first_decay).astype(BF)
    pair_local = apply(second_decay, first_local) + second_local.astype(F32)
    state = jnp.zeros_like(own_local)
    for turn in range(turns):
        state = pair_local if turn == 0 else apply(pair_decay, state) + pair_local
        state = shifted(state.astype(BF), 2)
    middle = (apply(first_decay, state) + first_local.astype(F32)).astype(BF)
    got = swapped(jnp.where(place == 0, middle, state), "fsdp", 1)
    entering = joined(jnp.where(place == 0, state, middle), got, place)
    return entering, (first_decay, second_decay, pair_decay)


def relay_backward(grads, maps):
    place = lax.axis_index("fsdp") % 2
    turns = lax.axis_size("fsdp") // 2 - 1
    first_decay, second_decay, pair_decay = maps
    own, send = halves(grads.astype(BF), place)
    got = swapped(send, "fsdp", 1)
    first_grad = jnp.where(place == 0, own, got)
    second_grad = jnp.where(place == 0, got, own)
    pair_grad = apply_back(first_decay, second_grad) + first_grad.astype(F32)
    state = jnp.zeros_like(own)
    for turn in range(turns):
        state = pair_grad if turn == 0 else apply_back(pair_decay, state) + pair_grad
        state = shifted(state.astype(BF), -2)
    middle = (apply_back(second_decay, state) + second_grad.astype(F32)).astype(BF)
    got = swapped(jnp.where(place == 0, state, middle), "fsdp", 1)
    return joined(jnp.where(place == 0, middle, state), got, place)


def inv_rms(values):
    return lax.rsqrt(jnp.mean(values * values, -1, keepdims=True) + EPS_NORM)


def flat_dot(pattern, left, right):
    return jnp.einsum(pattern, left, right, preferred_element_type=F32)


def padded(value, lanes):
    return jnp.pad(value, ((0, 0), (0, lanes - value.shape[1])))


def shards(
    layer_input_rows, sequence_lengths, attn_gain, qkv_weight, conv_weight, beta_weight,
    beta_bias, out_gain, out_weight, mlp_gain, gate_up_weight, down_weight, cotangent,
):
    row_count, seg_len, model = layer_input_rows.shape
    chain = lax.axis_size("fsdp")
    share = seg_len // 4
    place = lax.axis_index("tp")
    tap_count, _, heads, _ = conv_weight.shape
    width = 3 * heads * LANES
    wide = width + LANES
    hidden_count = down_weight.shape[0]
    slice_rows = model // chain
    head_slice = LANES // chain
    first = (lax.axis_index("fsdp") * seg_len).astype(jnp.int32).reshape(1)
    ends = jnp.cumsum(sequence_lengths, 1).astype(jnp.int32)
    bias = beta_bias.astype(F32)

    flat_qkv = jnp.concatenate(
        [qkv_weight.reshape(slice_rows, width), padded(beta_weight, LANES)], 1
    )
    small = jnp.concatenate(
        [attn_gain, mlp_gain, out_gain, conv_weight.reshape(-1)]
    )
    lead = -(-small.shape[0] // wide) * 16
    small = jnp.pad(small, (0, lead * wide - small.shape[0])).reshape(lead, wide)
    packed = lax.all_gather(jnp.concatenate([flat_qkv, small], 0), "fsdp", axis=0)
    weight = packed[:, :slice_rows].reshape(model, wide)
    small = packed[:, slice_rows:].reshape(chain, -1)
    attn_scale = small[:, :slice_rows].reshape(1, model).astype(F32)
    mlp_scale = small[:, slice_rows : 2 * slice_rows].reshape(1, model).astype(F32)
    at = 2 * slice_rows
    head_gain = small[:, at : at + head_slice].reshape(1, LANES).astype(F32)
    at += head_slice
    taps = small[:, at : at + tap_count * 3 * heads * head_slice]
    taps = taps.reshape(chain, tap_count, 3 * heads, head_slice).transpose(1, 2, 0, 3)
    taps = taps.reshape(tap_count, width).astype(F32)
    out_down = lax.all_gather(
        jnp.concatenate([out_weight.reshape(heads * LANES, slice_rows), down_weight], 0), "fsdp", axis=0
    )
    out_down = out_down.transpose(1, 0, 2).reshape(heads * LANES + hidden_count, model)
    out_full, down_full = out_down[: heads * LANES], out_down[heads * LANES :]
    gate_up_full = lax.all_gather(
        gate_up_weight.reshape(slice_rows, 2 * hidden_count), "fsdp", axis=0, tiled=True
    )

    rim = shifted(layer_input_rows[:, seg_len - RIM :], 1)
    normed_in, ext, query, local, inverse, decay, state_local = mix_forward(
        ends, first, bias, layer_input_rows, rim, attn_scale, weight, taps, heads
    )
    state_in, maps = relay_forward(decay, state_local)
    mixed, mixed_low, attn_part = head_forward(
        ends, first, query, local, state_in, head_gain, out_full
    )
    attn_own = tp_scatter(attn_part)
    own_input = lax.dynamic_slice_in_dim(layer_input_rows, place * share, share, 1).astype(F32)
    own_cot = lax.dynamic_slice_in_dim(cotangent, place * share, share, 1).astype(F32)
    residual = own_input + attn_own
    inv_second = inv_rms(residual)
    unit_second = residual * inv_second
    normed_mid = tp_gather((unit_second * mlp_scale).astype(BF))

    tokens = row_count * seg_len
    normed_mid = normed_mid.reshape(tokens, model)
    cot = cotangent.reshape(tokens, model)
    gate_up = flat_dot("td,df->tf", normed_mid, gate_up_full)
    gate, up = gate_up[:, :hidden_count], gate_up[:, hidden_count:]
    gate_sig = jax.nn.sigmoid(gate)
    gate_silu = gate * gate_sig
    hidden = (gate_silu * up).astype(BF)
    grad_hidden = flat_dot("td,fd->tf", cot, down_full)
    grad_gate = (grad_hidden * up * gate_sig * (1.0 + gate * (1.0 - gate_sig))).astype(BF)
    grad_up = (grad_hidden * gate_silu).astype(BF)
    grad_gate_up = jnp.concatenate([grad_gate, grad_up], 1)
    mid_part = flat_dot("tf,df->td", grad_gate_up, gate_up_full).astype(BF)
    grad_mid = tp_scatter(mid_part.reshape(row_count, seg_len, model))
    scaled = grad_mid * mlp_scale
    grad_residual = own_cot + inv_second * (
        scaled - unit_second * jnp.mean(scaled * unit_second, -1, keepdims=True)
    )
    mlp_gain_part = jnp.sum(grad_mid * unit_second, (0, 1))
    grad_attn = tp_gather(grad_residual.astype(BF))

    grad_mixed, grad_state, head_gain_grad = head_backward(
        ends, first, grad_attn, out_full, head_gain, mixed, query, heads
    )
    leave = relay_backward(grad_state, maps)
    grad_proj, tail, rim_grad, tap_grad, bias_grad = mix_backward(
        ends, first, bias, ext, taps, inverse, grad_mixed, state_in, leave
    )
    mlp_part = flat_dot("tf,fd->td", hidden, down_full).astype(BF)
    mlp_own = tp_scatter(mlp_part.reshape(row_count, seg_len, model))
    layer_output = (residual + mlp_own).astype(BF)
    rim_grad = shifted(rim_grad, -1)
    tail = (tail + rim_grad.astype(F32)).astype(BF)
    grad_proj = lax.dynamic_update_slice(grad_proj, tail, (0, seg_len - RIM, 0))
    flat_proj = grad_proj.reshape(tokens, wide)
    in_part = flat_dot("tf,df->td", flat_proj, weight).astype(BF)
    grad_in = tp_scatter(in_part.reshape(row_count, seg_len, model))
    inv_first = inv_rms(own_input)
    unit_first = own_input * inv_first
    attn_gain_part = jnp.sum(grad_in * unit_first, (0, 1))
    scaled = grad_in * attn_scale
    input_grad = grad_residual + inv_first * (
        scaled - unit_first * jnp.mean(scaled * unit_first, -1, keepdims=True)
    )

    flat_attn = grad_attn.reshape(tokens, model)
    grad_qkv = flat_dot("td,tf->df", normed_in.reshape(tokens, model), flat_proj).astype(BF)
    grad_gu = flat_dot("td,tf->df", normed_mid, grad_gate_up).astype(BF)
    grad_down = flat_dot("td,tf->df", cot, hidden).astype(BF)
    grad_out = flat_dot("td,tf->df", flat_attn, mixed_low.reshape(tokens, heads * LANES)).astype(BF)
    mlp_grads = lax.psum_scatter(
        jnp.concatenate([grad_gu, grad_down], 1), "fsdp", scatter_dimension=0, tiled=True
    )
    mix_grads = lax.psum_scatter(
        jnp.concatenate([grad_qkv, grad_out], 1), "fsdp", scatter_dimension=0, tiled=True
    )
    sums = jnp.concatenate([attn_gain_part, mlp_gain_part, head_gain_grad[0]])
    sums = lax.psum(lax.psum(sums, "fsdp"), "tp")
    segment = lax.axis_index("fsdp")
    attn_gain_grad = lax.dynamic_slice_in_dim(sums[:model], segment * slice_rows, slice_rows)
    mlp_gain_grad = lax.dynamic_slice_in_dim(sums[model : 2 * model], segment * slice_rows, slice_rows)
    out_gain_grad = lax.dynamic_slice_in_dim(sums[2 * model :], segment * head_slice, head_slice)
    tap_bias = lax.psum(jnp.concatenate([tap_grad[:tap_count], padded(bias_grad[:1], width)], 0), "fsdp")
    conv_grad = lax.dynamic_slice_in_dim(
        tap_bias[:tap_count].reshape(tap_count, 3, heads, LANES), segment * head_slice, head_slice, 3
    )
    mlp_grads = mlp_grads.astype(F32)
    mix_grads = mix_grads.astype(F32)
    return (
        layer_output,
        input_grad,
        attn_gain_grad,
        mix_grads[:, :width].reshape(slice_rows, 3, heads, LANES),
        conv_grad,
        mix_grads[:, width : width + heads],
        tap_bias[tap_count, :heads],
        out_gain_grad,
        mix_grads[:, wide:].T.reshape(heads, LANES, slice_rows),
        mlp_gain_grad,
        mlp_grads[:, : 2 * hidden_count].reshape(slice_rows, 2, hidden_count),
        mlp_grads[:, 2 * hidden_count :].T,
    )


def solution(mesh):
    in_specs = (
        P(None, "fsdp", None),
        P(),
        P("fsdp"),
        P("fsdp", None, "tp", None),
        P(None, None, "tp", "fsdp"),
        P("fsdp", "tp"),
        P("tp"),
        P("fsdp"),
        P("tp", None, "fsdp"),
        P("fsdp"),
        P("fsdp", None, "tp"),
        P("tp", "fsdp"),
        P(None, "fsdp", None),
    )
    out_specs = (
        P(None, ("fsdp", "tp"), None),
        P(None, ("fsdp", "tp"), None),
        P("fsdp"),
        P("fsdp", None, "tp", None),
        P(None, None, "tp", "fsdp"),
        P("fsdp", "tp"),
        P("tp"),
        P("fsdp"),
        P("tp", None, "fsdp"),
        P("fsdp"),
        P("fsdp", None, "tp"),
        P("tp", "fsdp"),
    )
    return jax.shard_map(shards, mesh=mesh, in_specs=in_specs, out_specs=out_specs, check_vma=False)
```

```python
import math

import jax
import jax.numpy as jnp
from jax import lax
from jax.experimental import pallas as pl
from jax.experimental.pallas import tpu as pltpu
from jax.sharding import PartitionSpec as P

BF = jnp.bfloat16
F32 = jnp.float32
EPS_NORM = 1e-05
EPS_UNIT = 1e-06
RIM = 16
LANES = 128
MIB = 60
BACK_STEP = 1


def dot(left, right):
    return lax.dot_general(left, right, (((1,), (0,)), ((), ())), preferred_element_type=F32)


def dot_nt(left, right):
    return lax.dot_general(left, right, (((1,), (1,)), ((), ())), preferred_element_type=F32)


def dot_tn(left, right):
    return lax.dot_general(left, right, (((0,), (0,)), ((), ())), preferred_element_type=F32)


def split(value):
    high = value.astype(BF)
    return high, (value - high.astype(F32)).astype(BF)


def left_pair(high, low):
    return jnp.concatenate([high, low], 1)


def right_pair(high, low):
    top = jnp.concatenate([high, low], 1)
    bottom = jnp.concatenate([high, jnp.zeros_like(low)], 1)
    return jnp.concatenate([top, bottom], 0)


def fold(both):
    half = both.shape[1] // 2
    return both[:, :half] + both[:, half:]


def doc_at(position, ends_ref, row):
    total = jnp.zeros_like(position)
    for slot in range(ends_ref.shape[1]):
        total = total + (position >= ends_ref[row, slot]).astype(jnp.int32)
    return total


def row_masks(ends_ref, first_ref, row, seg_len):
    first = first_ref[0]
    pos_cols = first + lax.broadcasted_iota(jnp.int32, (seg_len, LANES), 0)
    pos_rows = first + lax.broadcasted_iota(jnp.int32, (1, seg_len), 1)
    doc_cols = doc_at(pos_cols, ends_ref, row)
    doc_rows = doc_at(pos_rows, ends_ref, row)
    doc_before = doc_at(first - 1, ends_ref, row)
    doc_last = doc_at(first + seg_len - 1, ends_ref, row)
    entering = (doc_cols == doc_before).astype(F32)
    leaving = (doc_cols == doc_last).astype(F32)
    whole = (doc_before == doc_last).astype(F32)
    pad = (pos_cols < ends_ref[row, ends_ref.shape[1] - 1]).astype(F32)
    same = doc_cols[:, :1] == doc_rows
    return pos_cols, doc_cols, entering, leaving, whole, pad, same


def tap_masks(pos_cols, doc_cols, ends_ref, row, tap_count):
    return [None] + [
        (doc_at(pos_cols - tap, ends_ref, row) == doc_cols).astype(F32)
        for tap in range(1, tap_count)
    ]


def conv_tile(ext_ref, taps, tap_ref, lane, seg_len):
    cols = pl.ds(lane, LANES)
    total = tap_ref[0:1, cols] * ext_ref[pl.ds(RIM, seg_len), cols]
    for tap in range(1, len(taps)):
        total = total + tap_ref[tap : tap + 1, cols] * (
            ext_ref[pl.ds(RIM - tap, seg_len), cols] * taps[tap]
        )
    return total


def sigmoid(value):
    return 1.0 / (1.0 + jnp.exp(-value))


def triangle_inverses(lowers):
    size = lowers[0].shape[0]
    if size > LANES:
        half = size // 2
        tops = [lower[:half, :half] for lower in lowers]
        bottoms = [lower[half:, half:] for lower in lowers]
        done = triangle_inverses(tops + bottoms)
        tops, bottoms = done[: len(lowers)], done[len(lowers) :]
        across = [product3(end, lower[half:, :half]) for end, lower in zip(bottoms, lowers)]
        across = [product3(cross, top) for cross, top in zip(across, tops)]
        zeros = jnp.zeros((half, half), F32)
        return [
            jnp.concatenate(
                [jnp.concatenate([top, zeros], 1), jnp.concatenate([-cross, end], 1)], 0
            )
            for top, cross, end in zip(tops, across, bottoms)
        ]
    at_row = lax.broadcasted_iota(jnp.int32, (size, size), 0)
    at_col = lax.broadcasted_iota(jnp.int32, (size, size), 1)
    apart = at_row ^ at_col
    eye = (apart == 0).astype(F32)
    inverses = [eye - jnp.where(apart == 1, lower, 0.0) for lower in lowers]
    step = 1
    while (2 << step) <= size:
        inside = (apart >> step) == 1
        pairs = [split(inverse) for inverse in inverses]
        across = [
            fold(dot(left_pair(*pair), right_pair(*split(jnp.where(inside, lower, 0.0)))))
            for pair, lower in zip(pairs, lowers)
        ]
        across = [
            fold(dot(left_pair(*split(cross)), right_pair(*pair)))
            for cross, pair in zip(across, pairs)
        ]
        inverses = [inverse - cross for inverse, cross in zip(inverses, across)]
        step += 1
    return inverses


def product3(left, right):
    return fold(dot(left_pair(*split(left)), right_pair(*split(right))))


def row_sum(value):
    return dot(value.astype(BF), jnp.ones((value.shape[1], LANES), BF))


def in_turns(chains):
    chains = list(chains)
    while chains:
        chains = [chain for chain in chains if next(chain, chain) is not chain]


def extend_kernel(x_ref, rim_ref, out_ref):
    out_ref[:, pl.ds(0, RIM), :] = rim_ref[...]
    out_ref[:, pl.ds(RIM, x_ref.shape[1]), :] = x_ref[...]


def mix_kernel(
    ends_ref, first_ref, bias_ref, x_ref, gain_ref, w_ref, more_ref, tap_ref,
    normed_ref, ext_out_ref, query_ref, local_ref, inv_ref, decay_ref, state_ref,
):
    count, seg_len = query_ref.shape[:2]
    heads = inv_ref.shape[1]
    width = tap_ref.shape[1]
    at_row = lax.broadcasted_iota(jnp.int32, (seg_len, seg_len), 0)
    at_col = lax.broadcasted_iota(jnp.int32, (seg_len, seg_len), 1)
    eye = (
        lax.broadcasted_iota(jnp.int32, (LANES, LANES), 0)
        == lax.broadcasted_iota(jnp.int32, (LANES, LANES), 1)
    ).astype(F32)
    chains, lowers = [], []
    for at in range(count):
        row = pl.program_id(0) * count + at + first_ref[1]
        whole_x = x_ref[at].astype(F32)
        scale = lax.rsqrt(jnp.mean(whole_x * whole_x, -1, keepdims=True) + EPS_NORM)
        normed = (whole_x * scale * gain_ref[...]).astype(BF)
        normed_ref[at] = normed
        cut = w_ref.shape[1]
        rest = ext_out_ref.shape[2] - cut
        ext_out_ref[at, :, pl.ds(0, cut)] = dot(normed, w_ref[...])
        ext_out_ref[at, :, pl.ds(cut, rest)] = dot(normed, more_ref[:, pl.ds(0, rest)])
        masks = row_masks(ends_ref, first_ref, row, seg_len)
        taps = tap_masks(masks[0], masks[1], ends_ref, row, tap_ref.shape[0])
        for head in range(heads):
            chains.append((at, head, masks, taps))
    kept = []
    for at, head, masks, taps in chains:
        _, _, entering, leaving, whole, pad, same = masks
        ext = ext_out_ref.at[at]
        active = []
        for part in range(3):
            conv = conv_tile(ext, taps, tap_ref, (part * heads + head) * LANES, seg_len)
            active.append(conv * sigmoid(conv))
        query, key, value = active
        query = query * (
            lax.rsqrt(row_sum(query * query) + EPS_UNIT) * (1.0 / math.sqrt(LANES))
        )
        key = key * lax.rsqrt(row_sum(key * key) + EPS_UNIT)
        logit = ext[pl.ds(RIM, seg_len), pl.ds(width, LANES)][:, head : head + 1]
        rate = sigmoid(jnp.broadcast_to(logit, (seg_len, LANES)) + bias_ref[head]) * pad
        key_low = key.astype(BF)
        wide_rate = jnp.concatenate([rate] * (seg_len // LANES), 1)
        lowers.append(
            jnp.where(same & (at_row > at_col), wide_rate * dot_nt(key_low, key_low), 0.0)
        )
        right = jnp.concatenate([rate * entering * key, rate * value], 1).astype(BF)
        scores = jnp.where(
            same & (at_row >= at_col), dot_nt(query.astype(BF), key_low), 0.0
        ).astype(BF)
        kept.append((right, scores, entering * query, (leaving * key).astype(BF), whole * eye))
    inverses = triangle_inverses(lowers)

    def finish(at, head, inverse, right, scores, query, leaving_key, through):
        inverse = inverse.astype(BF)
        inv_ref[at, head] = inverse
        weighted = dot(inverse, right).astype(BF)
        yield
        mixed = dot(scores, weighted)
        ends_state = dot_tn(leaving_key, weighted)
        yield
        lanes = pl.ds(head * LANES, LANES)
        query_ref[at, :, lanes] = (query - mixed[:, :LANES]).astype(BF)
        local_ref[at, :, lanes] = mixed[:, LANES:]
        decay_ref[at, head] = (through - ends_state[:, :LANES]).astype(BF)
        state_ref[at, head] = ends_state[:, LANES:].astype(BF)

    in_turns(
        finish(chain[0], chain[1], inverse, *held)
        for chain, inverse, held in zip(chains, inverses, kept)
    )


def store_pieces(values_ref, slots_ref, refs, at):
    share = refs[0].shape[1]
    for index, ref in enumerate(refs):
        start = pl.multiple_of(slots_ref[index] * share, share)
        ref[at] = values_ref[pl.ds(start, share), :].astype(ref.dtype)


def load_pieces(values_ref, slots_ref, refs, at):
    share = refs[0].shape[1]
    for index, ref in enumerate(refs):
        start = pl.multiple_of(slots_ref[len(refs) - 1 - index] * share, share)
        values_ref[pl.ds(start, share), :] = ref[at]


def lay(pieces_ref, out_ref):
    @pl.when(pl.program_id(0) == 0)
    def _():
        step = pieces_ref.shape[2]
        if step % LANES:
            out_ref[...] = jnp.concatenate(
                [pieces_ref[at] for at in range(pieces_ref.shape[0])], 1
            )
        else:
            for at in range(pieces_ref.shape[0]):
                out_ref[:, pl.ds(at * step, step)] = pieces_ref[at]


def pad_mask(ends_ref, first_ref, row, seg_len):
    pos = first_ref[0] + lax.broadcasted_iota(jnp.int32, (seg_len, LANES), 0)
    return (pos < ends_ref[row, ends_ref.shape[1] - 1]).astype(F32)


def head_kernel(
    ends_ref, first_ref, slots_ref, query_ref, local_ref, state_ref, gain_ref, out_ref,
    mixed_ref, low_ref, piece0, piece1, piece2, piece3,
    attn_ref,
):
    wide = out_ref.shape[1] - low_ref.shape[2]
    count, seg_len = query_ref.shape[:2]
    heads = state_ref.shape[1]
    for at in range(count):
        row = pl.program_id(0) * count + at + first_ref[1]
        pad = pad_mask(ends_ref, first_ref, row, seg_len)
        for head in range(heads):
            lanes = pl.ds(head * LANES, LANES)
            mixed = local_ref[at, :, lanes] + dot(query_ref[at, :, lanes], state_ref[at, head])
            mixed_ref[at, :, lanes] = mixed
            scale = lax.rsqrt(jnp.mean(mixed * mixed, -1, keepdims=True) + EPS_NORM)
            low_ref[at, :, lanes] = (mixed * scale * gain_ref[...] * pad).astype(BF)
        attn_ref[at] = dot_nt(low_ref[at], out_ref[:, pl.ds(wide, low_ref.shape[2])])
        store_pieces(attn_ref.at[at], slots_ref, (piece0, piece1, piece2, piece3), at)


def middle_kernel(slots_ref, x_ref, piece_ref, near_ref, far_ref, gain_ref, residual_ref, normed_ref):
    residual = (
        x_ref[...].astype(F32) + piece_ref[...].astype(F32) + near_ref[...].astype(F32)
        + far_ref[...].astype(F32)
    )
    residual_ref[...] = residual
    scale = lax.rsqrt(jnp.mean(residual * residual, -1, keepdims=True) + EPS_NORM)
    normed_ref[...] = (residual * scale * gain_ref[...]).astype(BF)


def feed_kernel(
    slots_ref, own, far, core, both, cot_grad_ref, pieces_ref,
    normed_ref, hidden_ref, grads_ref, piece0, piece1, piece2, piece3,
    total_ref, w_ref,
):
    lay(pieces_ref, w_ref)
    width = hidden_ref.shape[2]
    chunk = 2 * LANES
    load_pieces(normed_ref.at[0], slots_ref, (own, far, core, both), 0)
    normed = normed_ref[0]
    for at in range(0, width, chunk):
        gate = dot_nt(normed, w_ref[pl.ds(at, chunk), :])
        up = dot_nt(normed, w_ref[pl.ds(width + at, chunk), :])
        grad = cot_grad_ref[0, :, pl.ds(at, chunk)]
        sig = sigmoid(gate)
        act = gate * sig
        hidden_ref[0, :, pl.ds(at, chunk)] = (act * up).astype(BF)
        grads_ref[0, :, pl.ds(at, chunk)] = (
            grad * up * (sig + act * (1.0 - sig))
        ).astype(BF)
        grads_ref[0, :, pl.ds(width + at, chunk)] = (grad * act).astype(BF)
    total_ref[...] = dot(grads_ref[0], w_ref[...])
    store_pieces(total_ref, slots_ref, (piece0, piece1, piece2, piece3), 0)


def middle_back_kernel(
    slots_ref, cot_ref, residual_ref, piece_ref, near_ref, far_ref, later_ref, gain_ref,
    grad_ref, low_ref, gain_grad_ref,
):
    @pl.when(pl.program_id(0) == 0)
    def _():
        gain_grad_ref[...] = jnp.zeros_like(gain_grad_ref)

    early = pl.program_id(0) < pl.num_programs(0) // 2
    for at in range(cot_ref.shape[0]):
        residual = residual_ref[at]
        scale = lax.rsqrt(jnp.mean(residual * residual, -1, keepdims=True) + EPS_NORM)
        unit = residual * scale
        far = jnp.where(early, far_ref[at], later_ref[at]).astype(F32)
        grad = piece_ref[at].astype(F32) + near_ref[at].astype(F32) + far
        gain_grad_ref[0:1, :] += jnp.sum(grad * unit, 0, keepdims=True)
        grad = grad * gain_ref[...]
        total = cot_ref[at].astype(F32) + scale * (
            grad - unit * jnp.mean(grad * unit, -1, keepdims=True)
        )
        grad_ref[at] = total
        low_ref[at] = total.astype(BF)


def first_back_kernel(
    slots_ref, x_ref, grad_ref, piece0, near0, far0, piece1, near1, far1, gain_ref, out_ref
):
    early = pl.program_id(0) < pl.num_programs(0) // 2
    values = x_ref[...].astype(F32)
    scale = lax.rsqrt(jnp.mean(values * values, -1, keepdims=True) + EPS_NORM)
    unit = values * scale
    grad = jnp.where(early, piece0[...], piece1[...]).astype(F32)
    grad = grad + jnp.where(early, near0[...], near1[...]).astype(F32)
    grad = grad + jnp.where(early, far0[...], far1[...]).astype(F32)
    grad = grad * gain_ref[...]
    out_ref[...] = grad_ref[...] + scale * (
        grad - unit * jnp.mean(grad * unit, -1, keepdims=True)
    )


def shared_kernel(slots_ref, x_ref, pieces_ref, piece0, piece1, piece2, piece3, total_ref, w_ref):
    lay(pieces_ref, w_ref)
    for at in range(x_ref.shape[0]):
        total_ref[at] = dot(x_ref[at], w_ref[...])
        store_pieces(total_ref.at[at], slots_ref, (piece0, piece1, piece2, piece3), at)


def cot_kernel(cot_ref, pieces_ref, out_ref, w_ref):
    lay(pieces_ref, w_ref)
    for at in range(cot_ref.shape[0]):
        out_ref[at] = dot_nt(cot_ref[at], w_ref[...])


def weight_grad_kernel(*refs):
    out_ref = refs[-1]
    pairs = len(refs) // 2 * 2 if len(refs) % 2 else len(refs) - 2
    total = 0.0
    for at in range(0, pairs, 2):
        left, right = refs[at], refs[at + 1]
        total = total + dot_tn(
            left[...].reshape(-1, left.shape[2]), right[...].reshape(-1, right.shape[2])
        )
    out_ref[...] = total.astype(BF)
    if len(refs) % 2 == 0:
        lanes = pl.ds(out_ref.shape[1] - LANES, LANES)
        out_ref[:, lanes] = out_ref[:, lanes] + refs[-2][...]


def project_back_kernel(
    slots_ref, grad_ref, tail_ref, rim_ref, w_ref, more_ref,
    piece0, piece1, piece2, piece3,
    fixed_ref, total_ref,
):
    count, seg_len = fixed_ref.shape[:2]
    width = tail_ref.shape[2]
    for at in range(count):
        fixed_ref[at] = grad_ref[at, pl.ds(RIM, seg_len), :]
        fixed_ref[at, pl.ds(seg_len - RIM, RIM), pl.ds(0, width)] = (
            tail_ref[at] + rim_ref[at].astype(F32)
        ).astype(BF)
        cut = w_ref.shape[1]
        rest = fixed_ref.shape[2] - cut
        total_ref[at] = dot_nt(fixed_ref[at, :, pl.ds(0, cut)], w_ref[...]) + dot_nt(
            fixed_ref[at, :, pl.ds(cut, rest)], more_ref[:, pl.ds(0, rest)]
        )
        store_pieces(total_ref.at[at], slots_ref, (piece0, piece1, piece2, piece3), at)


def head_back_kernel(
    ends_ref, first_ref, slots_ref, own, far, core, both, out_ref, gain_ref, mixed_ref, query_ref,
    grad_ref, grad_mixed_ref, state_ref, gain_grad_ref,
):
    wide = out_ref.shape[1] - query_ref.shape[2]
    count, seg_len = query_ref.shape[:2]
    heads = state_ref.shape[1]

    @pl.when(pl.program_id(0) == 0)
    def _():
        gain_grad_ref[...] = jnp.zeros_like(gain_grad_ref)

    for at in range(count):
        row = pl.program_id(0) * count + at + first_ref[1]
        pad = pad_mask(ends_ref, first_ref, row, seg_len)
        load_pieces(grad_ref.at[at], slots_ref, (own, far, core, both), at)
        grads = dot(grad_ref[at], out_ref[:, pl.ds(wide, query_ref.shape[2])])
        for head in range(heads):
            lanes = pl.ds(head * LANES, LANES)
            mixed = mixed_ref[at, :, lanes]
            scale = lax.rsqrt(jnp.mean(mixed * mixed, -1, keepdims=True) + EPS_NORM)
            unit = mixed * scale
            grad = grads[:, head * LANES : (head + 1) * LANES] * pad
            gain_grad_ref[0:1, :] += jnp.sum(grad * unit, 0, keepdims=True)
            grad = grad * gain_ref[...]
            grad = scale * (grad - unit * jnp.mean(grad * unit, -1, keepdims=True))
            low = grad.astype(BF)
            grad_mixed_ref[at, :, lanes] = low
            state_ref[at, head] = dot_tn(query_ref[at, :, lanes], low).astype(BF)


def mix_back_kernel(
    ends_ref, first_ref, bias_ref, ext_ref, tap_ref, inv_ref, grad_ref, state_ref, leave_ref,
    proj_ref, tail_ref, rim_ref, tap_grad_ref, bias_grad_ref,
    conv_ref,
):
    count, seg_len = grad_ref.shape[:2]
    heads = inv_ref.shape[1]
    width = tap_ref.shape[1]
    tap_count = tap_ref.shape[0]

    @pl.when(pl.program_id(0) == 0)
    def _():
        tap_grad_ref[...] = jnp.zeros_like(tap_grad_ref)
        bias_grad_ref[...] = jnp.zeros_like(bias_grad_ref)
        for at in range(count):
            conv_ref[at, pl.ds(0, RIM), :] = jnp.zeros((RIM, width), F32)
            conv_ref[at, pl.ds(RIM + seg_len, RIM), :] = jnp.zeros((RIM, width), F32)

    at_row = lax.broadcasted_iota(jnp.int32, (seg_len, seg_len), 0)
    at_col = lax.broadcasted_iota(jnp.int32, (seg_len, seg_len), 1)
    lane_at = lax.broadcasted_iota(jnp.int32, (seg_len, LANES), 1)
    rows = [pl.program_id(0) * count + at + first_ref[1] for at in range(count)]
    masks = [row_masks(ends_ref, first_ref, row, seg_len) for row in rows]
    all_taps = [
        tap_masks(mask[0], mask[1], ends_ref, row, tap_count) for mask, row in zip(masks, rows)
    ]
    logit_grads = [[] for _ in rows]

    def back(at, head):
        _, _, entering, leaving, _, pad, same = masks[at]
        strict = same & (at_row > at_col)
        causal = same & (at_row >= at_col)
        taps = all_taps[at]
        ext = ext_ref.at[at]
        convs, gates, active = [], [], []
        for part in range(3):
            conv = conv_tile(ext, taps, tap_ref, (part * heads + head) * LANES, seg_len)
            gate = sigmoid(conv)
            convs.append(conv)
            gates.append(gate)
            active.append(conv * gate)
        query_size = lax.rsqrt(row_sum(active[0] * active[0]) + EPS_UNIT)
        key_size = lax.rsqrt(row_sum(active[1] * active[1]) + EPS_UNIT)
        query_unit = active[0] * query_size
        key = active[1] * key_size
        value = active[2]
        logit = ext[pl.ds(RIM, seg_len), pl.ds(width, LANES)][:, head : head + 1]
        logit = jnp.broadcast_to(logit, (seg_len, LANES))
        gate_rate = sigmoid(logit + bias_ref[head])
        rate = gate_rate * pad
        query_low = (query_unit * (1.0 / math.sqrt(LANES))).astype(BF)
        key_low = key.astype(BF)
        state = state_ref[at, head]
        leave = leave_ref[at, head]
        inverse = inv_ref[at, head]
        lanes = pl.ds(head * LANES, LANES)
        grad = grad_ref[at, :, lanes]
        yield
        missing = value - entering * dot(key_low, state)
        yield
        fresh = dot(inverse, (rate * missing).astype(BF)).astype(BF)
        scores = jnp.where(causal, dot_nt(query_low, key_low), 0.0).astype(BF)
        yield
        leaving_key = (leaving * key).astype(BF)
        fresh_grad = dot_tn(scores, grad) + dot(leaving_key, leave)
        yield
        solved = dot_tn(inverse, fresh_grad.astype(BF))
        solved_low = solved.astype(BF)
        yield
        score_grad = jnp.where(causal, dot_nt(grad, fresh), 0.0).astype(BF)
        yield
        lower_grad = jnp.where(strict, -dot_nt(solved_low, fresh), 0.0)
        lower_low = lower_grad.astype(BF)
        rate_low = (jnp.concatenate([rate] * (seg_len // LANES), 1) * lower_grad).astype(BF)
        yield
        query_grad = entering * dot_nt(grad, state) + dot(score_grad, key_low)
        lower_key = dot(lower_low, key_low)
        yield
        value_grad = rate * solved
        key_grad = (
            dot_tn(score_grad, query_low)
            + leaving * dot_nt(fresh, leave)
            - entering * dot_nt(value_grad.astype(BF), state)
            + rate * lower_key
            + dot_tn(rate_low, key_low)
        )
        rate_grad = sum(row_sum(part) for part in split(solved * missing + key * lower_key))
        yield
        logit_grad = rate_grad * rate * (1.0 - gate_rate)
        logit_grads[at].append(jnp.where(lane_at == head, logit_grad, 0.0))
        query_grad = query_grad * (1.0 / math.sqrt(LANES))
        query_grad = query_size * (
            query_grad - query_unit * row_sum(query_unit * query_grad)
        )
        key_grad = key_size * (key_grad - key * row_sum(key * key_grad))
        for part, active_grad in enumerate((query_grad, key_grad, value_grad)):
            conv_grad = active_grad * (gates[part] * (1.0 + convs[part] * (1.0 - gates[part])))
            lane = (part * heads + head) * LANES
            cols = pl.ds(lane, LANES)
            conv_ref[at, pl.ds(RIM, seg_len), cols] = conv_grad
            for tap in range(tap_count):
                masked = conv_grad if tap == 0 else conv_grad * taps[tap]
                tap_grad_ref[tap : tap + 1, cols] += jnp.sum(
                    masked * ext[pl.ds(RIM - tap, seg_len), cols], 0, keepdims=True
                )

    in_turns(back(at, head) for at in range(count) for head in range(heads))
    pos_ext = first_ref[0] - RIM + lax.broadcasted_iota(jnp.int32, (seg_len + RIM, LANES), 0)
    for at, row in enumerate(rows):
        total = sum(logit_grads[at])
        bias_grad_ref[0:1, :] += jnp.sum(total, 0, keepdims=True)
        lanes = pl.ds(width, LANES)
        proj_ref[at, pl.ds(0, RIM), lanes] = jnp.zeros((RIM, LANES), BF)
        proj_ref[at, pl.ds(RIM, seg_len), lanes] = total.astype(BF)
        doc_ext = doc_at(pos_ext, ends_ref, row)
        back_masks = [None] + [
            (doc_at(pos_ext + tap, ends_ref, row) == doc_ext).astype(F32)
            for tap in range(1, tap_count)
        ]
        for lane in range(0, width, LANES):
            cols = pl.ds(lane, LANES)
            total = tap_ref[0:1, cols] * conv_ref[at, pl.ds(0, seg_len + RIM), cols]
            for tap in range(1, tap_count):
                total = total + tap_ref[tap : tap + 1, cols] * (
                    conv_ref[at, pl.ds(tap, seg_len + RIM), cols] * back_masks[tap]
                )
            rim_ref[at, :, cols] = total[:RIM].astype(BF)
            tail_ref[at, :, cols] = total[seg_len:]
            proj_ref[at, :, cols] = total.astype(BF)


def fixed(array):
    if isinstance(array, tuple):
        array, rows, block = array
        return pl.BlockSpec(
            (array.shape[0], rows, array.shape[2]), lambda *at: (0, block, 0)
        )
    return pl.BlockSpec(array.shape, lambda *at: (0,) * len(array.shape))


def shaped(shape, kind):
    return jax.ShapeDtypeStruct(shape, kind)


def limits(mib):
    return pltpu.CompilerParams(
        dimension_semantics=("arbitrary",), vmem_limit_bytes=mib << 20
    )


def no_cost():
    return pl.CostEstimate(flops=1, bytes_accessed=1, transcendentals=0)


def rows_of(array, step, start=0, own=False):
    shape = list(array.shape[1:])
    blocks = array.shape[0] // step
    if own == "early":
        return pl.BlockSpec(
            (step, *shape),
            lambda row, *scalars: (jnp.minimum(row, blocks - 1),) + (0,) * len(shape),
        )
    if own == "late":
        return pl.BlockSpec(
            (step, *shape),
            lambda row, *scalars: (jnp.maximum(row - blocks, 0),) + (0,) * len(shape),
        )
    if not own:
        return pl.BlockSpec(
            (step, *shape), lambda row, *scalars: (row + start // step,) + (0,) * len(shape)
        )
    shape[0] = shape[0] // 4
    return pl.BlockSpec(
        (step, *shape), lambda row, slots, *scalars: (row + start // step, slots[3], 0)
    )


def call(
    kernel, name, mib, count, step, scalars, by_row, whole, outs, sums=(), scratch=(), after=(),
    first_row=0, into=(),
):
    lead = len(scalars)
    skip = len(after) + len(into)

    def body(*refs):
        kernel(*refs[:lead], *refs[lead + skip :])

    outs, sums = list(outs), list(sums)
    by_row = [item if isinstance(item, tuple) else (item, 0, False) for item in by_row]
    return pl.pallas_call(
        body,
        grid_spec=pltpu.PrefetchScalarGridSpec(
            num_scalar_prefetch=lead,
            grid=(count // step,),
            in_specs=[pl.BlockSpec(memory_space=pl.ANY) for _ in (*after, *into)]
            + [rows_of(array, step, start, own) for array, start, own in by_row]
            + [fixed(array) for array in whole],
            out_specs=[rows_of(array, step, first_row) for array in outs]
            + [fixed(array) for array in sums],
            scratch_shapes=list(scratch),
        ),
        out_shape=outs + sums,
        compiler_params=limits(mib),
        cost_estimate=no_cost(),
        input_output_aliases={lead + len(after) + at: at for at in range(len(into))},
        name=name,
    )(*scalars, *after, *into, *[item[0] for item in by_row],
      *[item[0] if isinstance(item, tuple) else item for item in whole])


def extend(rows, rim, after=()):
    count, seg_len, model = rows.shape
    return call(
        extend_kernel, "extend", MIB, count, 2, (), (rows, rim), (),
        [shaped((count, seg_len + RIM, model), BF)], after=after,
    )[0]


def mix_forward(ends, first, bias, rows, start, count, gain, weights, taps, heads, after=()):
    seg_len, model = rows.shape[1] - RIM, rows.shape[2]
    both = heads * LANES
    wide = weights[0].shape[1] + weights[1].shape[1] - both
    return call(
        mix_kernel, "mix_forward", MIB, count, min(2, count), (ends, first, bias),
        ((rows, start, False),),
        (gain, *weights, taps),
        (
            shaped((count, seg_len + RIM, model), BF),
            shaped((count, seg_len + RIM, wide), F32),
            shaped((count, seg_len, both), BF),
            shaped((count, seg_len, both), F32),
            shaped((count, heads, seg_len, seg_len), BF),
            shaped((count, heads, LANES, LANES), BF),
            shaped((count, heads, LANES, LANES), BF),
        ),
        after=after,
    )


def piece_shapes(count, share, model):
    return [shaped((count, share, model), BF)] * 4


def head_forward(
    ends, first, slots, query, local, state, start, count, gain, out_full, after=()
):
    seg_len, both = query.shape[1:]
    model = out_full.shape[0]
    step = min(2, count)
    outs = call(
        head_kernel, "head_forward", MIB, count, step, (ends, first, slots),
        [(array, start, False) for array in (query, local, state)], (gain, out_full),
        [shaped((count, seg_len, both), F32), shaped((count, seg_len, both), BF)]
        + piece_shapes(count, seg_len // 4, model),
        scratch=[pltpu.VMEM((step, seg_len, model), F32)], after=after,
    )
    return outs[0], outs[1], outs[2:]


def middle_forward(slots, rows, start, pieces, gain, after=()):
    count, share, model = pieces[0].shape
    return call(
        middle_kernel, "middle_forward", MIB, count, min(4, count), (slots,),
        ((rows, start, True), *pieces), (gain,),
        (shaped((count, share, model), F32), shaped((count, share, model), BF)), after=after,
    )


def feed_forward(slots, pieces, cot_grad, weight, after=()):
    count, seg_len, width = cot_grad.shape
    share, model = pieces[0].shape[1:]
    outs = call(
        feed_kernel, "feed_forward", MIB, count, 1, (slots,), (*pieces, cot_grad), (weight,),
        [
            shaped((count, seg_len, model), BF), shaped((count, seg_len, width), BF),
            shaped((count, seg_len, 2 * width), BF),
        ] + piece_shapes(count, share, model),
        scratch=[pltpu.VMEM((seg_len, model), F32), pltpu.VMEM((2 * width, model), BF)],
        after=after,
    )
    return outs[0], outs[1], outs[2], outs[3:]


def middle_backward(slots, cot, start, residual, pieces, gain, after=()):
    count, share, model = residual.shape
    return call(
        middle_back_kernel, "middle_backward", MIB, count, count // 2, (slots,),
        (
            (cot, start, True), residual, *pieces[:2], (pieces[2], 0, "early"),
            (pieces[3], 0, "late"),
        ),
        (gain,),
        (shaped((count, share, model), F32), shaped((count, share, model), BF)),
        sums=[shaped((8, model), F32)], after=after,
    )


def first_backward(slots, rows, start, grad, pieces, later, gain, after=()):
    count, share, model = grad.shape
    return call(
        first_back_kernel, "first_backward", MIB, count, count // 2, (slots,),
        (
            (rows, start, True), grad, *[(piece, 0, "early") for piece in pieces],
            *[(piece, 0, "late") for piece in later],
        ),
        (gain,), [shaped((count, share, model), F32)], after=after,
    )[0]


def shared_product(slots, values, weight, after=()):
    count, seg_len, depth = values.shape
    model = weight[0].shape[0] * weight[0].shape[2]
    step = min(2, count)
    return call(
        shared_kernel, "shared_product", MIB, count, step, (slots,), (values,), (weight,),
        piece_shapes(count, seg_len // 4, model),
        scratch=[pltpu.VMEM((step, seg_len, model), F32), pltpu.VMEM((depth, model), BF)],
        after=after,
    )


def cot_backward(cot, start, count, weight, width, after=()):
    seg_len, model = cot.shape[1:]
    return call(
        cot_kernel, "cot_backward", MIB, count, 2, (),
        ((cot, start, False),), (weight,),
        [shaped((count, seg_len, width), F32)], scratch=[pltpu.VMEM((width, model), BF)],
        after=after,
    )[0]


def weight_grad(lefts, rights, extra=None, after=()):
    lefts = [item if isinstance(item, tuple) else (item, 0) for item in lefts]
    model, width = lefts[0][0].shape[2], rights[0].shape[2]
    tile = 2 * LANES
    ins, specs = [], []
    for (left, start), right in zip(lefts, rights):
        ins += [left, right]
        count, depth = right.shape[:2]
        specs += [
            pl.BlockSpec(
                (count, depth, tile), lambda at, block=start // count: (block, 0, at)
            ),
            fixed(right),
        ]
    if extra is not None:
        ins.append(extra)
        specs.append(pl.BlockSpec((tile, LANES), lambda at: (at, 0)))

    def body(*refs):
        weight_grad_kernel(*refs[len(after) :])

    return pl.pallas_call(
        body,
        grid=(model // tile,),
        in_specs=[pl.BlockSpec(memory_space=pl.ANY) for _ in after] + specs,
        out_specs=pl.BlockSpec((tile, width), lambda at: (at, 0)),
        out_shape=shaped((model, width), BF),
        compiler_params=limits(MIB),
        cost_estimate=no_cost(),
        name="weight_grad",
    )(*after, *ins)


def finish_kernel(grad_ref, w_ref, gain_ref, qkv_ref, rest_ref, sum_ref):
    parts, heads = qkv_ref.shape[1:3]
    width = parts * heads * LANES
    values = grad_ref[...].astype(F32)
    for part in range(parts):
        for head in range(heads):
            at = (part * heads + head) * LANES
            qkv_ref[:, part, head, :] = values[:, at : at + LANES]
    rest = values[:, width:]
    rest_ref[...] = rest
    used = lax.broadcasted_iota(jnp.int32, rest.shape, 1) < heads
    weight = w_ref[...].astype(F32)
    total = jnp.sum(weight[:, :width] * values[:, :width], 1, keepdims=True)
    total = total + jnp.sum(jnp.where(used, weight[:, width:] * rest, 0.0), 1, keepdims=True)
    sum_ref[...] = jnp.broadcast_to(total / gain_ref[...], sum_ref.shape)


def finish(grads, weight, gain, heads):
    rows = grads.shape[0]
    outs = [
        shaped((rows, 3, heads, LANES), F32), shaped((rows, LANES), F32), shaped((rows, LANES), F32)
    ]
    ins = (grads, weight, gain)
    return pl.pallas_call(
        finish_kernel,
        grid=(1,),
        in_specs=[fixed(array) for array in ins],
        out_specs=[fixed(out) for out in outs],
        out_shape=outs,
        compiler_params=limits(MIB),
        cost_estimate=no_cost(),
        name="finish",
    )(*ins)


def settle_kernel(gu_ref, down_ref, gu_out, down_out, out_out):
    hidden = gu_out.shape[1]
    half = gu_ref.shape[1] // 2
    flat = gu_ref[...].astype(F32).T
    gu_out[0] = flat[:hidden]
    gu_out[1] = flat[half : half + hidden]
    flat = down_ref[...].astype(F32).T
    down_out[...] = flat[:hidden]
    out_out[...] = flat[half:].reshape(out_out.shape)


def settle(gu_grads, down_out, hidden, heads, after=()):
    rows = gu_grads.shape[0]

    def body(*refs):
        settle_kernel(*refs[len(after) :])

    outs = [
        shaped((2, hidden, rows), F32), shaped((hidden, rows), F32),
        shaped((heads, LANES, rows), F32),
    ]
    return pl.pallas_call(
        body,
        grid=(1,),
        in_specs=[pl.BlockSpec(memory_space=pl.ANY) for _ in after]
        + [fixed(gu_grads), fixed(down_out)],
        out_specs=[fixed(out) for out in outs],
        out_shape=outs,
        compiler_params=limits(MIB),
        cost_estimate=no_cost(),
        name="settle",
    )(*after, gu_grads, down_out)


def fence(values, tokens):
    count = len(values)
    anywhere = pl.BlockSpec(memory_space=pl.ANY)
    return pl.pallas_call(
        lambda *refs: None,
        in_specs=[anywhere] * (count + len(tokens)),
        out_specs=[anywhere] * count,
        out_shape=[shaped(value.shape, value.dtype) for value in values],
        input_output_aliases={at: at for at in range(count)},
        cost_estimate=no_cost(),
        name="fence",
    )(*values, *tokens)


def project_backward(slots, grad, tail, rim, start, count, weights, after=()):
    seg_len = grad.shape[1] - RIM
    model = weights[0].shape[0]
    step = min(2, count)
    return call(
        project_back_kernel, "project_backward", MIB, count, step, (slots,),
        [(array, start, False) for array in (grad, tail, rim)],
        weights, piece_shapes(count, seg_len // 4, model),
        scratch=[
            pltpu.VMEM((step, seg_len, grad.shape[2]), BF), pltpu.VMEM((step, seg_len, model), F32)
        ],
        after=after,
    )


def head_backward(
    ends, first, slots, pieces, out_full, gain, mixed, query, start, heads, after=()
):
    count, model = pieces[0].shape[0], pieces[0].shape[2]
    seg_len, both = query.shape[1:]
    return call(
        lambda ends_ref, first_ref, slots_ref, own, far, core, side, mixed_ref, query_ref,
        out_ref, gain_ref, *outs: head_back_kernel(
            ends_ref, first_ref, slots_ref, own, far, core, side, out_ref, gain_ref, mixed_ref,
            query_ref, *outs
        ),
        "head_backward", MIB, count, min(2, count), (ends, first, slots),
        (*pieces, mixed, (query, start, False)),
        (out_full, gain),
        (
            shaped((count, seg_len, model), BF),
            shaped((count, seg_len, both), BF),
            shaped((count, heads, LANES, LANES), BF),
        ),
        sums=[shaped((8, LANES), F32)], after=after,
    )


def mix_backward(
    ends, first, bias, ext, taps, inverse, grad, state, leave, start, share, after=(), into=()
):
    count, seg_len, both = grad.shape
    wide = ext.shape[2]
    tap_count, width = taps.shape
    return call(
        lambda ends_ref, first_ref, bias_ref, ext_ref, inv_ref, grad_ref, state_ref, leave_ref,
        tap_ref, *rest: mix_back_kernel(
            ends_ref, first_ref, bias_ref, ext_ref, tap_ref, inv_ref, grad_ref, state_ref,
            leave_ref, *rest
        ),
        "mix_backward", MIB, share, BACK_STEP, (ends, first, bias),
        [(array, start, False) for array in (ext, inverse, grad, state, leave)], (taps,),
        (
            shaped((count, seg_len + RIM, wide), BF),
            shaped((count, RIM, width), F32),
            shaped((count, RIM, width), BF),
        ),
        sums=[shaped((8, width), F32), shaped((8, LANES), F32)],
        scratch=[pltpu.VMEM((BACK_STEP, seg_len + 2 * RIM, width), F32)], after=after, first_row=start,
        into=into,
    )


def shifted(value, distance):
    devices = range(lax.axis_size("fsdp"))
    route = [(i - distance, i) for i in devices if i - distance in devices]
    return lax.ppermute(value, "fsdp", route)


def swapped(value, axis, bit):
    return lax.ppermute(value, axis, [(i, i ^ bit) for i in range(lax.axis_size(axis))])


def pick(value, index, axis):
    return lax.dynamic_index_in_dim(value, index, axis, keepdims=False)


def core_sums(pieces, *tokens):
    other_far, other_own, own_far, own = pieces
    got_far = swapped(other_far, "tp", 1)
    got_own = swapped(other_own, "tp", 1)
    got_far = held(got_far, *tokens) if tokens else got_far
    return (own_far.astype(F32) + got_far.astype(F32)).astype(BF), own, got_own


def held(value, *tokens):
    return fence((value,), tokens)[0]


def across(value):
    return swapped(value, "tp", 2)


def beside_core(value):
    return swapped(value, "tp", 1)


def sides():
    return [list(range(at, lax.axis_size("fsdp"), 2)) for at in (0, 1)]


def two_step_gather(own):
    side = lax.axis_index("fsdp") % 2
    mine = lax.all_gather(own, "fsdp", axis=0, axis_index_groups=sides())
    other = swapped(mine, "fsdp", 1)
    return jnp.stack([jnp.where(side == 0, mine, other), jnp.where(side == 0, other, mine)], 1)


def pair_parts(parts, *tokens):
    count = lax.axis_size("fsdp") // 2
    side = lax.axis_index("fsdp") % 2
    view = parts.reshape(count, 2, -1, parts.shape[1])
    return pick(view, side, 1), behind(pick(view, 1 - side, 1), *tokens)


def line_scatter(sums):
    return lax.psum_scatter(
        sums.astype(BF).reshape(-1, sums.shape[-1]), "fsdp", scatter_dimension=0, tiled=True,
        axis_index_groups=sides(),
    )


def doubled_gather(own):
    bit = 1
    index = lax.axis_index("fsdp")
    while bit < lax.axis_size("fsdp"):
        other = swapped(own, "fsdp", bit)
        first = (index & bit) == 0
        own = jnp.concatenate([jnp.where(first, own, other), jnp.where(first, other, own)], 0)
        bit *= 2
    return own


def behind(value, *tokens):
    for token in tokens:
        value = value + (token[(0,) * token.ndim].astype(F32) * 0.0).astype(value.dtype)
    return value


def summed(value, axis):
    bit = 1
    while bit < lax.axis_size(axis):
        value = value + swapped(value, axis, bit)
        bit *= 2
    return value


def apply(maps, states):
    return jnp.einsum("rhij,rhjk->rhik", maps, states, preferred_element_type=F32)


def apply_back(maps, states):
    return jnp.einsum("rhji,rhjk->rhik", maps, states, preferred_element_type=F32)


def halves(value, place):
    count = value.shape[0] // 2
    pair = value.reshape((2, count) + value.shape[1:])
    return pick(pair, place, 0), pick(pair, 1 - place, 0)


def joined(kept, got, place):
    first = jnp.where(place == 0, kept, got)
    second = jnp.where(place == 0, got, kept)
    return jnp.concatenate([first, second], 0)


def relay_forward(decay, local, tokens=()):
    place = lax.axis_index("fsdp") % 2
    turns = lax.axis_size("fsdp") // 2 - 1
    own_decay, send_decay = halves(decay, place)
    own_local, send_local = halves(local, place)
    got_decay, got_local = swapped((send_decay, send_local), "fsdp", 1)
    first_decay = jnp.where(place == 0, own_decay, got_decay)
    first_local = jnp.where(place == 0, own_local, got_local)
    second_decay = jnp.where(place == 0, got_decay, own_decay)
    second_local = jnp.where(place == 0, got_local, own_local)
    pair_decay = apply(second_decay, first_decay).astype(BF)
    pair_local = apply(second_decay, first_local) + second_local.astype(F32)
    state = jnp.zeros_like(own_local)
    for turn in range(turns):
        state = pair_local if turn == 0 else apply(pair_decay, state) + pair_local
        state = behind(state, *tokens[turn]) if turn < len(tokens) else state
        state = shifted(state.astype(BF), 2)
        early_state = state if turn <= max(turns - 2, 0) else early_state
    middle = (apply(first_decay, state) + first_local.astype(F32)).astype(BF)
    got = swapped(jnp.where(place == 0, middle, state), "fsdp", 1)
    entering = joined(jnp.where(place == 0, state, middle), got, place)
    return entering, early_state, (first_decay, second_decay, pair_decay)


def relay_backward(grads, maps, *beside):
    place = lax.axis_index("fsdp") % 2
    turns = lax.axis_size("fsdp") // 2 - 1
    first_decay, second_decay, pair_decay = maps
    beside = list(beside)

    def sent(transfer, value):
        got = transfer(value)
        return held(got, *beside.pop(0)(value)) if beside else got

    own, send = halves(grads, place)
    got = sent(lambda value: swapped(value, "fsdp", 1), send)
    first_grad = jnp.where(place == 0, own, got)
    second_grad = jnp.where(place == 0, got, own)
    pair_grad = apply_back(first_decay, second_grad) + first_grad.astype(F32)
    state = jnp.zeros_like(own)
    for turn in range(turns):
        state = pair_grad if turn == 0 else apply_back(pair_decay, state) + pair_grad
        state = sent(lambda value: shifted(value, -2), state.astype(BF))
    middle = (apply_back(second_decay, state) + second_grad.astype(F32)).astype(BF)
    got = swapped(jnp.where(place == 0, state, middle), "fsdp", 1)
    return joined(jnp.where(place == 0, middle, state), got, place)


def padded(value, lanes):
    return jnp.pad(value, ((0, 0), (0, lanes - value.shape[1])))


def shards(
    layer_input_rows, sequence_lengths, attn_gain, qkv_weight, conv_weight, beta_weight,
    beta_bias, out_gain, out_weight, mlp_gain, gate_up_weight, down_weight, cotangent,
):
    row_count, seg_len, model = layer_input_rows.shape
    chain = lax.axis_size("fsdp")
    place = lax.axis_index("tp")
    segment = lax.axis_index("fsdp")
    tap_count, _, heads, _ = conv_weight.shape
    width = 3 * heads * LANES
    wide = width + LANES
    both = heads * LANES
    hidden_count = down_weight.shape[0]
    hidden_wide = -(-hidden_count // (2 * LANES)) * 2 * LANES
    slice_rows = model // chain
    head_slice = LANES // chain
    first = (segment * seg_len).astype(jnp.int32)
    ends = jnp.cumsum(sequence_lengths, 1).astype(jnp.int32)
    bias = beta_bias.astype(F32)
    near, far = place % 2, place // 2
    slots = jnp.stack(
        [2 * (1 - far) + 1 - near, 2 * far + 1 - near, 2 * (1 - far) + near, 2 * far + near]
    ).astype(jnp.int32)
    first = jnp.stack([first, jnp.int32(0)])

    rim = shifted(layer_input_rows[:, seg_len - RIM :], 1)
    block = padded(beta_weight, LANES)
    flat_qkv = jnp.concatenate([qkv_weight.reshape(slice_rows, width), block], 1)
    cut = flat_qkv.shape[1] * 4 // 7
    more = jnp.concatenate([flat_qkv[:, cut:], out_weight.reshape(both, slice_rows).T], 1)
    weight = lax.all_gather(flat_qkv[:, :cut], "fsdp", axis=0, tiled=True)
    more = two_step_gather(more).reshape(model, -1)
    small = jnp.concatenate([attn_gain, mlp_gain, out_gain, conv_weight.reshape(-1)])
    small = doubled_gather(jnp.pad(small, (0, -small.shape[0] % LANES)).reshape(1, -1))
    attn_scale = small[:, :slice_rows].reshape(1, model).astype(F32)
    mlp_scale = small[:, slice_rows : 2 * slice_rows].reshape(1, model).astype(F32)
    at = 2 * slice_rows
    head_gain = small[:, at : at + head_slice].reshape(1, LANES).astype(F32)
    at += head_slice
    taps = small[:, at : at + tap_count * 3 * heads * head_slice]
    taps = taps.reshape(chain, tap_count, 3 * heads, head_slice).transpose(1, 2, 0, 3)
    taps = taps.reshape(tap_count, width).astype(F32)
    extended = extend(
        layer_input_rows, rim, after=(attn_scale, mlp_scale, head_gain, taps, ends)
    )
    extra = hidden_wide - hidden_count
    weights = (held(weight, extended, more), more)
    gate_up_flip = jnp.pad(gate_up_weight.transpose(1, 2, 0), ((0, 0), (0, extra), (0, 0)))
    feed_weight = jnp.concatenate(
        [
            gate_up_flip.reshape(2 * hidden_wide, slice_rows),
            jnp.pad(down_weight, ((0, extra), (0, 0))),
        ],
        0,
    )

    normed_in, ext, query, local, inverse, decay, state_local = mix_forward(
        ends, first, bias, extended, 0, row_count, attn_scale, weights, taps, heads
    )
    state_in, early_state, maps = relay_forward(decay, state_local)
    feed_weight = lax.all_gather(held(feed_weight, early_state), "fsdp", axis=0)
    gate_up_full, down_full = (feed_weight, 2 * hidden_wide, 0), (feed_weight, hidden_wide, 2)
    mixed, mixed_low, pieces = head_forward(
        ends, first, slots, query, local, state_in, 0, row_count, head_gain, weights[1]
    )
    crossing, kept, near = core_sums(pieces)
    far = across(crossing)
    residual, own = middle_forward(slots, layer_input_rows, 0, (kept, near, far), mlp_scale)
    near, far = beside_core(own), across(own)
    cot_grad = cot_backward(cotangent, 0, row_count, down_full, hidden_wide, after=(own,))
    far = held(far, cot_grad)
    normed_mid, hidden, grad_gate_up, pieces = feed_forward(
        slots, (own, far, near, beside_core(far)), cot_grad, gate_up_full
    )
    crossing, kept, near = core_sums(pieces)
    half = row_count // 2
    grad_gu = weight_grad((normed_mid,), (grad_gate_up,), after=(crossing[:half],))
    far = held(across(crossing[:half]), grad_gu)
    gu_grads = lax.psum_scatter(held(grad_gu, far), "fsdp", scatter_dimension=0, tiled=True)
    grad_down = weight_grad(((cotangent, 0),), (hidden,), after=(far,))
    later = held(across(held(crossing[half:], far)), grad_down)
    grad_residual, own, mlp_gain_part = middle_backward(
        slots, cotangent, 0, residual, (kept, near, far, later), mlp_scale
    )
    near, far = beside_core(own), across(own)
    output = shared_product(slots, hidden, down_full, after=(own,))
    far = held(far, output[0])
    grad_attn, grad_mixed, grad_state, head_gain_part = head_backward(
        ends, first, slots, (own, far, near, beside_core(far)), weights[1], head_gain, mixed, query,
        0, heads,
    )

    done = []

    def out_beside(value):
        done.append(weight_grad((grad_attn,), (mixed_low,), after=(value,)))
        done.append(jnp.concatenate([grad_down, done[0]], 1))
        return (done[1],)

    def sums_beside(value):
        done.append(core_sums(fence(output, (value,))))
        return (done[2][0],)

    leave = relay_backward(grad_state, maps, out_beside, sums_beside)
    _, down_out, (crossing, kept, near) = done
    far = across(crossing)
    down_out = held(down_out, leave)
    grad_proj, tail, rim_grad, tap_part, bias_part = mix_backward(
        ends, first, bias, ext, taps, inverse, grad_mixed, state_in, leave, 0, row_count,
        after=(down_out,),
    )
    far = held(far, grad_proj)
    layer_output = sum((part.astype(F32) for part in (kept, near, far)), residual).astype(BF)
    down_out = lax.psum_scatter(down_out, "fsdp", scatter_dimension=0, tiled=True)
    rim_back = shifted(rim_grad, -1)

    tap_grad = tap_part[:tap_count].reshape(tap_count * 3 * heads, chain, head_slice)
    tap_grad = tap_grad.transpose(1, 0, 2).reshape(chain, -1)
    small = [
        mlp_gain_part[0].reshape(chain, slice_rows), head_gain_part[0].reshape(chain, head_slice),
        tap_grad,
    ]
    small = jnp.concatenate(small, 1)
    lanes = -(-small.shape[1] // slice_rows)
    small = jnp.pad(small, ((0, 0), (0, lanes * slice_rows - small.shape[1])))
    small = small.reshape(chain, lanes, slice_rows).transpose(0, 2, 1).reshape(model, lanes)
    terms = jnp.stack(split(bias_part[0, :heads]), 1)
    own_lanes = (jnp.arange(chain) == segment).astype(BF)
    terms = (own_lanes[:, None] * terms[:, None, :]).reshape(heads, 2 * chain)
    terms = jnp.pad(terms, ((0, slice_rows - heads), (0, 0)))
    small = jnp.concatenate([small.astype(BF), jnp.tile(terms, (chain, 1))], 1)
    small = jnp.pad(small, ((0, 0), (heads, LANES - heads - small.shape[1])))
    grad_qkv = weight_grad((normed_in,), (grad_proj,), extra=small)
    own_part, sent = pair_parts(grad_qkv, rim_back)
    pieces = project_backward(
        slots, grad_proj, tail, rim_back, 0, half, weights, after=(sent, gu_grads, far)
    )
    crossing, kept, near = core_sums(pieces)
    terms_a = (kept, near, across(crossing))
    pieces = project_backward(
        slots, grad_proj, tail, rim_back, half, half, weights, after=(crossing,)
    )
    got = held(swapped(sent, "fsdp", 1), pieces[0], down_out)
    crossing, kept, near = core_sums(pieces)
    qkv_grads = line_scatter(own_part.astype(F32) + got.astype(F32))
    gate_up_grad, down_grad, out_weight_grad = settle(
        gu_grads, down_out, hidden_count, heads, after=(crossing,)
    )
    terms_b = (kept, near, held(across(crossing), gate_up_grad, layer_output))
    input_grad = first_backward(
        slots, layer_input_rows, 0, grad_residual, terms_a, terms_b, attn_scale,
        after=(gate_up_grad,),
    )
    qkv_grads = held(qkv_grads, gate_up_grad, layer_output)
    qkv_grad, rest_grad, gain_terms = finish(
        qkv_grads, flat_qkv, attn_gain.astype(F32).reshape(slice_rows, 1), heads
    )
    small = rest_grad[:, heads : heads + lanes].T.reshape(-1)
    over_tp = jnp.concatenate([gain_terms[:, 0], small[: slice_rows + head_slice]])
    over_tp = jnp.pad(over_tp, (0, -over_tp.shape[0] % LANES)).reshape(-1, LANES)
    over_tp = summed(over_tp, "tp").reshape(-1)
    at = slice_rows + head_slice
    bias_grad = jnp.sum(
        rest_grad[:heads, heads + lanes : heads + lanes + 2 * chain], 1
    )
    conv_grad = small[at : at + tap_count * 3 * heads * head_slice]
    return (
        layer_output,
        input_grad,
        over_tp[:slice_rows],
        qkv_grad,
        conv_grad.reshape(tap_count, 3, heads, head_slice),
        rest_grad[:, :heads],
        bias_grad,
        over_tp[2 * slice_rows : 2 * slice_rows + head_slice],
        out_weight_grad,
        over_tp[slice_rows : 2 * slice_rows],
        gate_up_grad.transpose(2, 0, 1),
        down_grad,
    )


def solution(mesh):
    in_specs = (
        P(None, "fsdp", None),
        P(),
        P("fsdp"),
        P("fsdp", None, "tp", None),
        P(None, None, "tp", "fsdp"),
        P("fsdp", "tp"),
        P("tp"),
        P("fsdp"),
        P("tp", None, "fsdp"),
        P("fsdp"),
        P("fsdp", None, "tp"),
        P("tp", "fsdp"),
        P(None, "fsdp", None),
    )
    out_specs = (
        P(None, ("fsdp", "tp"), None),
        P(None, ("fsdp", "tp"), None),
        P("fsdp"),
        P("fsdp", None, "tp", None),
        P(None, None, "tp", "fsdp"),
        P("fsdp", "tp"),
        P("tp"),
        P("fsdp"),
        P("tp", None, "fsdp"),
        P("fsdp"),
        P("fsdp", None, "tp"),
        P("tp", "fsdp"),
    )
    return jax.shard_map(shards, mesh=mesh, in_specs=in_specs, out_specs=out_specs, check_vma=False)
```

```python
import math

import jax
import jax.numpy as jnp
from jax import lax
from jax.experimental import pallas as pl
from jax.experimental.pallas import tpu as pltpu
from jax.sharding import PartitionSpec as P

BF = jnp.bfloat16
F32 = jnp.float32
EPS_NORM = 1e-05
EPS_UNIT = 1e-06
RIM = 16
LANES = 128
MIB = 60
BACK_STEP = 1


def dot(left, right):
    return lax.dot_general(left, right, (((1,), (0,)), ((), ())), preferred_element_type=F32)


def dot_nt(left, right):
    return lax.dot_general(left, right, (((1,), (1,)), ((), ())), preferred_element_type=F32)


def dot_tn(left, right):
    return lax.dot_general(left, right, (((0,), (0,)), ((), ())), preferred_element_type=F32)


def split(value):
    high = value.astype(BF)
    return high, (value - high.astype(F32)).astype(BF)


def left_pair(high, low):
    return jnp.concatenate([high, low], 1)


def right_pair(high, low):
    top = jnp.concatenate([high, low], 1)
    bottom = jnp.concatenate([high, jnp.zeros_like(low)], 1)
    return jnp.concatenate([top, bottom], 0)


def fold(both):
    half = both.shape[1] // 2
    return both[:, :half] + both[:, half:]


def doc_at(position, ends_ref, row):
    total = jnp.zeros_like(position)
    for slot in range(ends_ref.shape[1]):
        total = total + (position >= ends_ref[row, slot]).astype(jnp.int32)
    return total


def row_masks(ends_ref, first_ref, row, seg_len):
    first = first_ref[0]
    pos_cols = first + lax.broadcasted_iota(jnp.int32, (seg_len, LANES), 0)
    pos_rows = first + lax.broadcasted_iota(jnp.int32, (1, seg_len), 1)
    doc_cols = doc_at(pos_cols, ends_ref, row)
    doc_rows = doc_at(pos_rows, ends_ref, row)
    doc_before = doc_at(first - 1, ends_ref, row)
    doc_last = doc_at(first + seg_len - 1, ends_ref, row)
    entering = (doc_cols == doc_before).astype(F32)
    leaving = (doc_cols == doc_last).astype(F32)
    whole = (doc_before == doc_last).astype(F32)
    pad = (pos_cols < ends_ref[row, ends_ref.shape[1] - 1]).astype(F32)
    same = doc_cols[:, :1] == doc_rows
    return pos_cols, doc_cols, entering, leaving, whole, pad, same


def tap_masks(pos_cols, doc_cols, ends_ref, row, tap_count):
    return [None] + [
        (doc_at(pos_cols - tap, ends_ref, row) == doc_cols).astype(F32)
        for tap in range(1, tap_count)
    ]


def conv_tile(ext_ref, taps, tap_ref, lane, seg_len):
    cols = pl.ds(lane, LANES)
    total = tap_ref[0:1, cols] * ext_ref[pl.ds(RIM, seg_len), cols]
    for tap in range(1, len(taps)):
        total = total + tap_ref[tap : tap + 1, cols] * (
            ext_ref[pl.ds(RIM - tap, seg_len), cols] * taps[tap]
        )
    return total


def sigmoid(value):
    return 1.0 / (1.0 + jnp.exp(-value))


def triangle_inverses(lowers):
    size = lowers[0].shape[0]
    if size > LANES:
        half = size // 2
        tops = [lower[:half, :half] for lower in lowers]
        bottoms = [lower[half:, half:] for lower in lowers]
        done = triangle_inverses(tops + bottoms)
        tops, bottoms = done[: len(lowers)], done[len(lowers) :]
        across = [product3(end, lower[half:, :half]) for end, lower in zip(bottoms, lowers)]
        across = [product3(cross, top) for cross, top in zip(across, tops)]
        zeros = jnp.zeros((half, half), F32)
        return [
            jnp.concatenate(
                [jnp.concatenate([top, zeros], 1), jnp.concatenate([-cross, end], 1)], 0
            )
            for top, cross, end in zip(tops, across, bottoms)
        ]
    at_row = lax.broadcasted_iota(jnp.int32, (size, size), 0)
    at_col = lax.broadcasted_iota(jnp.int32, (size, size), 1)
    apart = at_row ^ at_col
    eye = (apart == 0).astype(F32)
    inverses = [eye - jnp.where(apart == 1, lower, 0.0) for lower in lowers]
    step = 1
    while (2 << step) <= size:
        inside = (apart >> step) == 1
        pairs = [split(inverse) for inverse in inverses]
        across = [
            fold(dot(left_pair(*pair), right_pair(*split(jnp.where(inside, lower, 0.0)))))
            for pair, lower in zip(pairs, lowers)
        ]
        across = [
            fold(dot(left_pair(*split(cross)), right_pair(*pair)))
            for cross, pair in zip(across, pairs)
        ]
        inverses = [inverse - cross for inverse, cross in zip(inverses, across)]
        step += 1
    return inverses


def product3(left, right):
    return fold(dot(left_pair(*split(left)), right_pair(*split(right))))


def row_sum(value):
    return dot(value.astype(BF), jnp.ones((value.shape[1], LANES), BF))


def in_turns(chains):
    chains = list(chains)
    while chains:
        chains = [chain for chain in chains if next(chain, chain) is not chain]


def extend_kernel(x_ref, rim_ref, out_ref):
    out_ref[:, pl.ds(0, RIM), :] = rim_ref[...]
    out_ref[:, pl.ds(RIM, x_ref.shape[1]), :] = x_ref[...]


def mix_kernel(
    ends_ref, first_ref, bias_ref, x_ref, gain_ref, w_ref, more_ref, tap_ref,
    normed_ref, ext_out_ref, query_ref, local_ref, inv_ref, decay_ref, state_ref,
):
    count, seg_len = query_ref.shape[:2]
    heads = inv_ref.shape[1]
    width = tap_ref.shape[1]
    at_row = lax.broadcasted_iota(jnp.int32, (seg_len, seg_len), 0)
    at_col = lax.broadcasted_iota(jnp.int32, (seg_len, seg_len), 1)
    eye = (
        lax.broadcasted_iota(jnp.int32, (LANES, LANES), 0)
        == lax.broadcasted_iota(jnp.int32, (LANES, LANES), 1)
    ).astype(F32)
    chains, lowers = [], []
    for at in range(count):
        row = pl.program_id(0) * count + at + first_ref[1]
        whole_x = x_ref[at].astype(F32)
        scale = lax.rsqrt(jnp.mean(whole_x * whole_x, -1, keepdims=True) + EPS_NORM)
        normed = (whole_x * scale * gain_ref[...]).astype(BF)
        normed_ref[at] = normed
        cut = w_ref.shape[1]
        rest = ext_out_ref.shape[2] - cut
        ext_out_ref[at, :, pl.ds(0, cut)] = dot(normed, w_ref[...])
        ext_out_ref[at, :, pl.ds(cut, rest)] = dot(normed, more_ref[:, pl.ds(0, rest)])
        masks = row_masks(ends_ref, first_ref, row, seg_len)
        taps = tap_masks(masks[0], masks[1], ends_ref, row, tap_ref.shape[0])
        for head in range(heads):
            chains.append((at, head, masks, taps))
    kept = []
    for at, head, masks, taps in chains:
        _, _, entering, leaving, whole, pad, same = masks
        ext = ext_out_ref.at[at]
        active = []
        for part in range(3):
            conv = conv_tile(ext, taps, tap_ref, (part * heads + head) * LANES, seg_len)
            active.append(conv * sigmoid(conv))
        query, key, value = active
        query = query * (
            lax.rsqrt(row_sum(query * query) + EPS_UNIT) * (1.0 / math.sqrt(LANES))
        )
        key = key * lax.rsqrt(row_sum(key * key) + EPS_UNIT)
        logit = ext[pl.ds(RIM, seg_len), pl.ds(width, LANES)][:, head : head + 1]
        rate = sigmoid(jnp.broadcast_to(logit, (seg_len, LANES)) + bias_ref[head]) * pad
        key_low = key.astype(BF)
        wide_rate = jnp.concatenate([rate] * (seg_len // LANES), 1)
        lowers.append(
            jnp.where(same & (at_row > at_col), wide_rate * dot_nt(key_low, key_low), 0.0)
        )
        right = jnp.concatenate([rate * entering * key, rate * value], 1).astype(BF)
        scores = jnp.where(
            same & (at_row >= at_col), dot_nt(query.astype(BF), key_low), 0.0
        ).astype(BF)
        kept.append((right, scores, entering * query, (leaving * key).astype(BF), whole * eye))
    inverses = triangle_inverses(lowers)

    def finish(at, head, inverse, right, scores, query, leaving_key, through):
        inverse = inverse.astype(BF)
        inv_ref[at, head] = inverse
        weighted = dot(inverse, right).astype(BF)
        yield
        mixed = dot(scores, weighted)
        ends_state = dot_tn(leaving_key, weighted)
        yield
        lanes = pl.ds(head * LANES, LANES)
        query_ref[at, :, lanes] = (query - mixed[:, :LANES]).astype(BF)
        local_ref[at, :, lanes] = mixed[:, LANES:]
        decay_ref[at, head] = (through - ends_state[:, :LANES]).astype(BF)
        state_ref[at, head] = ends_state[:, LANES:].astype(BF)

    in_turns(
        finish(chain[0], chain[1], inverse, *held)
        for chain, inverse, held in zip(chains, inverses, kept)
    )


def store_pieces(values_ref, slots_ref, refs, at):
    share = refs[0].shape[1]
    for index, ref in enumerate(refs):
        start = pl.multiple_of(slots_ref[index] * share, share)
        ref[at] = values_ref[pl.ds(start, share), :].astype(ref.dtype)


def load_pieces(values_ref, slots_ref, refs, at):
    share = refs[0].shape[1]
    for index, ref in enumerate(refs):
        start = pl.multiple_of(slots_ref[len(refs) - 1 - index] * share, share)
        values_ref[pl.ds(start, share), :] = ref[at]


def lay(pieces_ref, out_ref):
    @pl.when(pl.program_id(0) == 0)
    def _():
        step = pieces_ref.shape[2]
        if step % LANES:
            out_ref[...] = jnp.concatenate(
                [pieces_ref[at] for at in range(pieces_ref.shape[0])], 1
            )
        else:
            for at in range(pieces_ref.shape[0]):
                out_ref[:, pl.ds(at * step, step)] = pieces_ref[at]


def pad_mask(ends_ref, first_ref, row, seg_len):
    pos = first_ref[0] + lax.broadcasted_iota(jnp.int32, (seg_len, LANES), 0)
    return (pos < ends_ref[row, ends_ref.shape[1] - 1]).astype(F32)


def head_kernel(
    ends_ref, first_ref, slots_ref, query_ref, local_ref, state_ref, gain_ref, out_ref,
    mixed_ref, low_ref, piece0, piece1, piece2, piece3,
    attn_ref,
):
    wide = out_ref.shape[1] - low_ref.shape[2]
    count, seg_len = query_ref.shape[:2]
    heads = state_ref.shape[1]
    for at in range(count):
        row = pl.program_id(0) * count + at + first_ref[1]
        pad = pad_mask(ends_ref, first_ref, row, seg_len)
        for head in range(heads):
            lanes = pl.ds(head * LANES, LANES)
            mixed = local_ref[at, :, lanes] + dot(query_ref[at, :, lanes], state_ref[at, head])
            mixed_ref[at, :, lanes] = mixed
            scale = lax.rsqrt(jnp.mean(mixed * mixed, -1, keepdims=True) + EPS_NORM)
            low_ref[at, :, lanes] = (mixed * scale * gain_ref[...] * pad).astype(BF)
        attn_ref[at] = dot_nt(low_ref[at], out_ref[:, pl.ds(wide, low_ref.shape[2])])
        store_pieces(attn_ref.at[at], slots_ref, (piece0, piece1, piece2, piece3), at)


def middle_kernel(slots_ref, x_ref, piece_ref, near_ref, far_ref, gain_ref, residual_ref, normed_ref):
    residual = (
        x_ref[...].astype(F32) + piece_ref[...].astype(F32) + near_ref[...].astype(F32)
        + far_ref[...].astype(F32)
    )
    residual_ref[...] = residual
    scale = lax.rsqrt(jnp.mean(residual * residual, -1, keepdims=True) + EPS_NORM)
    normed_ref[...] = (residual * scale * gain_ref[...]).astype(BF)


def feed_kernel(
    slots_ref, own, far, core, both, cot_grad_ref, pieces_ref,
    normed_ref, hidden_ref, grads_ref, piece0, piece1, piece2, piece3,
    total_ref, w_ref,
):
    lay(pieces_ref, w_ref)
    width = hidden_ref.shape[2]
    chunk = 2 * LANES
    load_pieces(normed_ref.at[0], slots_ref, (own, far, core, both), 0)
    normed = normed_ref[0]
    for at in range(0, width, chunk):
        gate = dot_nt(normed, w_ref[pl.ds(at, chunk), :])
        up = dot_nt(normed, w_ref[pl.ds(width + at, chunk), :])
        grad = cot_grad_ref[0, :, pl.ds(at, chunk)]
        sig = sigmoid(gate)
        act = gate * sig
        hidden_ref[0, :, pl.ds(at, chunk)] = (act * up).astype(BF)
        grads_ref[0, :, pl.ds(at, chunk)] = (
            grad * up * (sig + act * (1.0 - sig))
        ).astype(BF)
        grads_ref[0, :, pl.ds(width + at, chunk)] = (grad * act).astype(BF)
    total_ref[...] = dot(grads_ref[0], w_ref[...])
    store_pieces(total_ref, slots_ref, (piece0, piece1, piece2, piece3), 0)


def middle_back_kernel(
    slots_ref, cot_ref, residual_ref, piece_ref, near_ref, far_ref, later_ref, gain_ref,
    grad_ref, low_ref, gain_grad_ref,
):
    @pl.when(pl.program_id(0) == 0)
    def _():
        gain_grad_ref[...] = jnp.zeros_like(gain_grad_ref)

    early = pl.program_id(0) < pl.num_programs(0) // 2
    for at in range(cot_ref.shape[0]):
        residual = residual_ref[at]
        scale = lax.rsqrt(jnp.mean(residual * residual, -1, keepdims=True) + EPS_NORM)
        unit = residual * scale
        far = jnp.where(early, far_ref[at], later_ref[at]).astype(F32)
        grad = piece_ref[at].astype(F32) + near_ref[at].astype(F32) + far
        gain_grad_ref[0:1, :] += jnp.sum(grad * unit, 0, keepdims=True)
        grad = grad * gain_ref[...]
        total = cot_ref[at].astype(F32) + scale * (
            grad - unit * jnp.mean(grad * unit, -1, keepdims=True)
        )
        grad_ref[at] = total
        low_ref[at] = total.astype(BF)


def first_back_kernel(
    slots_ref, x_ref, grad_ref, piece0, near0, far0, piece1, near1, far1, gain_ref, out_ref
):
    early = pl.program_id(0) < pl.num_programs(0) // 2
    values = x_ref[...].astype(F32)
    scale = lax.rsqrt(jnp.mean(values * values, -1, keepdims=True) + EPS_NORM)
    unit = values * scale
    grad = jnp.where(early, piece0[...], piece1[...]).astype(F32)
    grad = grad + jnp.where(early, near0[...], near1[...]).astype(F32)
    grad = grad + jnp.where(early, far0[...], far1[...]).astype(F32)
    grad = grad * gain_ref[...]
    out_ref[...] = grad_ref[...] + scale * (
        grad - unit * jnp.mean(grad * unit, -1, keepdims=True)
    )


def shared_kernel(slots_ref, x_ref, pieces_ref, piece0, piece1, piece2, piece3, total_ref, w_ref):
    lay(pieces_ref, w_ref)
    for at in range(x_ref.shape[0]):
        total_ref[at] = dot(x_ref[at], w_ref[...])
        store_pieces(total_ref.at[at], slots_ref, (piece0, piece1, piece2, piece3), at)


def cot_kernel(cot_ref, pieces_ref, out_ref, w_ref):
    lay(pieces_ref, w_ref)
    for at in range(cot_ref.shape[0]):
        out_ref[at] = dot_nt(cot_ref[at], w_ref[...])


def weight_grad_kernel(*refs):
    out_ref = refs[-1]
    pairs = len(refs) // 2 * 2 if len(refs) % 2 else len(refs) - 2
    total = 0.0
    for at in range(0, pairs, 2):
        left, right = refs[at], refs[at + 1]
        total = total + dot_tn(
            left[...].reshape(-1, left.shape[2]), right[...].reshape(-1, right.shape[2])
        )
    out_ref[...] = total.astype(BF)
    if len(refs) % 2 == 0:
        lanes = pl.ds(out_ref.shape[1] - LANES, LANES)
        out_ref[:, lanes] = out_ref[:, lanes] + refs[-2][...]


def project_back_kernel(
    slots_ref, grad_ref, tail_ref, rim_ref, w_ref, more_ref,
    piece0, piece1, piece2, piece3,
    fixed_ref, total_ref,
):
    count, seg_len = fixed_ref.shape[:2]
    width = tail_ref.shape[2]
    for at in range(count):
        fixed_ref[at] = grad_ref[at, pl.ds(RIM, seg_len), :]
        fixed_ref[at, pl.ds(seg_len - RIM, RIM), pl.ds(0, width)] = (
            tail_ref[at] + rim_ref[at].astype(F32)
        ).astype(BF)
        cut = w_ref.shape[1]
        rest = fixed_ref.shape[2] - cut
        total_ref[at] = dot_nt(fixed_ref[at, :, pl.ds(0, cut)], w_ref[...]) + dot_nt(
            fixed_ref[at, :, pl.ds(cut, rest)], more_ref[:, pl.ds(0, rest)]
        )
        store_pieces(total_ref.at[at], slots_ref, (piece0, piece1, piece2, piece3), at)


def head_back_kernel(
    ends_ref, first_ref, slots_ref, own, far, core, both, out_ref, gain_ref, mixed_ref, query_ref,
    grad_ref, grad_mixed_ref, state_ref, gain_grad_ref,
):
    wide = out_ref.shape[1] - query_ref.shape[2]
    count, seg_len = query_ref.shape[:2]
    heads = state_ref.shape[1]

    @pl.when(pl.program_id(0) == 0)
    def _():
        gain_grad_ref[...] = jnp.zeros_like(gain_grad_ref)

    for at in range(count):
        row = pl.program_id(0) * count + at + first_ref[1]
        pad = pad_mask(ends_ref, first_ref, row, seg_len)
        load_pieces(grad_ref.at[at], slots_ref, (own, far, core, both), at)
        grads = dot(grad_ref[at], out_ref[:, pl.ds(wide, query_ref.shape[2])])
        for head in range(heads):
            lanes = pl.ds(head * LANES, LANES)
            mixed = mixed_ref[at, :, lanes]
            scale = lax.rsqrt(jnp.mean(mixed * mixed, -1, keepdims=True) + EPS_NORM)
            unit = mixed * scale
            grad = grads[:, head * LANES : (head + 1) * LANES] * pad
            gain_grad_ref[0:1, :] += jnp.sum(grad * unit, 0, keepdims=True)
            grad = grad * gain_ref[...]
            grad = scale * (grad - unit * jnp.mean(grad * unit, -1, keepdims=True))
            low = grad.astype(BF)
            grad_mixed_ref[at, :, lanes] = low
            state_ref[at, head] = dot_tn(query_ref[at, :, lanes], low).astype(BF)


def mix_back_kernel(
    ends_ref, first_ref, bias_ref, ext_ref, tap_ref, inv_ref, grad_ref, state_ref, leave_ref,
    proj_ref, tail_ref, rim_ref, tap_grad_ref, bias_grad_ref,
    conv_ref,
):
    count, seg_len = grad_ref.shape[:2]
    heads = inv_ref.shape[1]
    width = tap_ref.shape[1]
    tap_count = tap_ref.shape[0]

    @pl.when(pl.program_id(0) == 0)
    def _():
        tap_grad_ref[...] = jnp.zeros_like(tap_grad_ref)
        bias_grad_ref[...] = jnp.zeros_like(bias_grad_ref)
        for at in range(count):
            conv_ref[at, pl.ds(0, RIM), :] = jnp.zeros((RIM, width), F32)
            conv_ref[at, pl.ds(RIM + seg_len, RIM), :] = jnp.zeros((RIM, width), F32)

    at_row = lax.broadcasted_iota(jnp.int32, (seg_len, seg_len), 0)
    at_col = lax.broadcasted_iota(jnp.int32, (seg_len, seg_len), 1)
    lane_at = lax.broadcasted_iota(jnp.int32, (seg_len, LANES), 1)
    rows = [pl.program_id(0) * count + at + first_ref[1] for at in range(count)]
    masks = [row_masks(ends_ref, first_ref, row, seg_len) for row in rows]
    all_taps = [
        tap_masks(mask[0], mask[1], ends_ref, row, tap_count) for mask, row in zip(masks, rows)
    ]
    logit_grads = [[] for _ in rows]

    def back(at, head):
        _, _, entering, leaving, _, pad, same = masks[at]
        strict = same & (at_row > at_col)
        causal = same & (at_row >= at_col)
        taps = all_taps[at]
        ext = ext_ref.at[at]
        convs, gates, active = [], [], []
        for part in range(3):
            conv = conv_tile(ext, taps, tap_ref, (part * heads + head) * LANES, seg_len)
            gate = sigmoid(conv)
            convs.append(conv)
            gates.append(gate)
            active.append(conv * gate)
        query_size = lax.rsqrt(row_sum(active[0] * active[0]) + EPS_UNIT)
        key_size = lax.rsqrt(row_sum(active[1] * active[1]) + EPS_UNIT)
        query_unit = active[0] * query_size
        key = active[1] * key_size
        value = active[2]
        logit = ext[pl.ds(RIM, seg_len), pl.ds(width, LANES)][:, head : head + 1]
        logit = jnp.broadcast_to(logit, (seg_len, LANES))
        gate_rate = sigmoid(logit + bias_ref[head])
        rate = gate_rate * pad
        query_low = (query_unit * (1.0 / math.sqrt(LANES))).astype(BF)
        key_low = key.astype(BF)
        state = state_ref[at, head]
        leave = leave_ref[at, head]
        inverse = inv_ref[at, head]
        lanes = pl.ds(head * LANES, LANES)
        grad = grad_ref[at, :, lanes]
        yield
        missing = value - entering * dot(key_low, state)
        yield
        fresh = dot(inverse, (rate * missing).astype(BF)).astype(BF)
        scores = jnp.where(causal, dot_nt(query_low, key_low), 0.0).astype(BF)
        yield
        leaving_key = (leaving * key).astype(BF)
        fresh_grad = dot_tn(scores, grad) + dot(leaving_key, leave)
        yield
        solved = dot_tn(inverse, fresh_grad.astype(BF))
        solved_low = solved.astype(BF)
        yield
        score_grad = jnp.where(causal, dot_nt(grad, fresh), 0.0).astype(BF)
        yield
        lower_grad = jnp.where(strict, -dot_nt(solved_low, fresh), 0.0)
        lower_low = lower_grad.astype(BF)
        rate_low = (jnp.concatenate([rate] * (seg_len // LANES), 1) * lower_grad).astype(BF)
        yield
        query_grad = entering * dot_nt(grad, state) + dot(score_grad, key_low)
        lower_key = dot(lower_low, key_low)
        yield
        value_grad = rate * solved
        key_grad = (
            dot_tn(score_grad, query_low)
            + leaving * dot_nt(fresh, leave)
            - entering * dot_nt(value_grad.astype(BF), state)
            + rate * lower_key
            + dot_tn(rate_low, key_low)
        )
        rate_grad = sum(row_sum(part) for part in split(solved * missing + key * lower_key))
        yield
        logit_grad = rate_grad * rate * (1.0 - gate_rate)
        logit_grads[at].append(jnp.where(lane_at == head, logit_grad, 0.0))
        query_grad = query_grad * (1.0 / math.sqrt(LANES))
        query_grad = query_size * (
            query_grad - query_unit * row_sum(query_unit * query_grad)
        )
        key_grad = key_size * (key_grad - key * row_sum(key * key_grad))
        for part, active_grad in enumerate((query_grad, key_grad, value_grad)):
            conv_grad = active_grad * (gates[part] * (1.0 + convs[part] * (1.0 - gates[part])))
            lane = (part * heads + head) * LANES
            cols = pl.ds(lane, LANES)
            conv_ref[at, pl.ds(RIM, seg_len), cols] = conv_grad
            for tap in range(tap_count):
                masked = conv_grad if tap == 0 else conv_grad * taps[tap]
                tap_grad_ref[tap : tap + 1, cols] += jnp.sum(
                    masked * ext[pl.ds(RIM - tap, seg_len), cols], 0, keepdims=True
                )

    in_turns(back(at, head) for at in range(count) for head in range(heads))
    pos_ext = first_ref[0] - RIM + lax.broadcasted_iota(jnp.int32, (seg_len + RIM, LANES), 0)
    for at, row in enumerate(rows):
        total = sum(logit_grads[at])
        bias_grad_ref[0:1, :] += jnp.sum(total, 0, keepdims=True)
        lanes = pl.ds(width, LANES)
        proj_ref[at, pl.ds(0, RIM), lanes] = jnp.zeros((RIM, LANES), BF)
        proj_ref[at, pl.ds(RIM, seg_len), lanes] = total.astype(BF)
        doc_ext = doc_at(pos_ext, ends_ref, row)
        back_masks = [None] + [
            (doc_at(pos_ext + tap, ends_ref, row) == doc_ext).astype(F32)
            for tap in range(1, tap_count)
        ]
        for lane in range(0, width, LANES):
            cols = pl.ds(lane, LANES)
            total = tap_ref[0:1, cols] * conv_ref[at, pl.ds(0, seg_len + RIM), cols]
            for tap in range(1, tap_count):
                total = total + tap_ref[tap : tap + 1, cols] * (
                    conv_ref[at, pl.ds(tap, seg_len + RIM), cols] * back_masks[tap]
                )
            rim_ref[at, :, cols] = total[:RIM].astype(BF)
            tail_ref[at, :, cols] = total[seg_len:]
            proj_ref[at, :, cols] = total.astype(BF)


def fixed(array):
    if isinstance(array, tuple):
        array, rows, block = array
        return pl.BlockSpec(
            (array.shape[0], rows, array.shape[2]), lambda *at: (0, block, 0)
        )
    return pl.BlockSpec(array.shape, lambda *at: (0,) * len(array.shape))


def shaped(shape, kind):
    return jax.ShapeDtypeStruct(shape, kind)


def limits(mib):
    return pltpu.CompilerParams(
        dimension_semantics=("arbitrary",), vmem_limit_bytes=mib << 20
    )


def no_cost():
    return pl.CostEstimate(flops=1, bytes_accessed=1, transcendentals=0)


def rows_of(array, step, start=0, own=False):
    shape = list(array.shape[1:])
    blocks = array.shape[0] // step
    if own == "early":
        return pl.BlockSpec(
            (step, *shape),
            lambda row, *scalars: (jnp.minimum(row, blocks - 1),) + (0,) * len(shape),
        )
    if own == "late":
        return pl.BlockSpec(
            (step, *shape),
            lambda row, *scalars: (jnp.maximum(row - blocks, 0),) + (0,) * len(shape),
        )
    if not own:
        return pl.BlockSpec(
            (step, *shape), lambda row, *scalars: (row + start // step,) + (0,) * len(shape)
        )
    shape[0] = shape[0] // 4
    return pl.BlockSpec(
        (step, *shape), lambda row, slots, *scalars: (row + start // step, slots[3], 0)
    )


def call(
    kernel, name, mib, count, step, scalars, by_row, whole, outs, sums=(), scratch=(), after=(),
    first_row=0, into=(),
):
    lead = len(scalars)
    skip = len(after) + len(into)

    def body(*refs):
        kernel(*refs[:lead], *refs[lead + skip :])

    outs, sums = list(outs), list(sums)
    by_row = [item if isinstance(item, tuple) else (item, 0, False) for item in by_row]
    return pl.pallas_call(
        body,
        grid_spec=pltpu.PrefetchScalarGridSpec(
            num_scalar_prefetch=lead,
            grid=(count // step,),
            in_specs=[pl.BlockSpec(memory_space=pl.ANY) for _ in (*after, *into)]
            + [rows_of(array, step, start, own) for array, start, own in by_row]
            + [fixed(array) for array in whole],
            out_specs=[rows_of(array, step, first_row) for array in outs]
            + [fixed(array) for array in sums],
            scratch_shapes=list(scratch),
        ),
        out_shape=outs + sums,
        compiler_params=limits(mib),
        cost_estimate=no_cost(),
        input_output_aliases={lead + len(after) + at: at for at in range(len(into))},
        name=name,
    )(*scalars, *after, *into, *[item[0] for item in by_row],
      *[item[0] if isinstance(item, tuple) else item for item in whole])


def extend(rows, rim, after=()):
    count, seg_len, model = rows.shape
    return call(
        extend_kernel, "extend", MIB, count, 2, (), (rows, rim), (),
        [shaped((count, seg_len + RIM, model), BF)], after=after,
    )[0]


def mix_forward(ends, first, bias, rows, start, count, gain, weights, taps, heads, after=()):
    seg_len, model = rows.shape[1] - RIM, rows.shape[2]
    both = heads * LANES
    wide = weights[0].shape[1] + weights[1].shape[1] - both
    return call(
        mix_kernel, "mix_forward", MIB, count, min(2, count), (ends, first, bias),
        ((rows, start, False),),
        (gain, *weights, taps),
        (
            shaped((count, seg_len + RIM, model), BF),
            shaped((count, seg_len + RIM, wide), F32),
            shaped((count, seg_len, both), BF),
            shaped((count, seg_len, both), F32),
            shaped((count, heads, seg_len, seg_len), BF),
            shaped((count, heads, LANES, LANES), BF),
            shaped((count, heads, LANES, LANES), BF),
        ),
        after=after,
    )


def piece_shapes(count, share, model):
    return [shaped((count, share, model), BF)] * 4


def head_forward(
    ends, first, slots, query, local, state, start, count, gain, out_full, after=()
):
    seg_len, both = query.shape[1:]
    model = out_full.shape[0]
    step = min(2, count)
    outs = call(
        head_kernel, "head_forward", MIB, count, step, (ends, first, slots),
        [(array, start, False) for array in (query, local, state)], (gain, out_full),
        [shaped((count, seg_len, both), F32), shaped((count, seg_len, both), BF)]
        + piece_shapes(count, seg_len // 4, model),
        scratch=[pltpu.VMEM((step, seg_len, model), F32)], after=after,
    )
    return outs[0], outs[1], outs[2:]


def middle_forward(slots, rows, start, pieces, gain, after=()):
    count, share, model = pieces[0].shape
    return call(
        middle_kernel, "middle_forward", MIB, count, min(4, count), (slots,),
        ((rows, start, True), *pieces), (gain,),
        (shaped((count, share, model), F32), shaped((count, share, model), BF)), after=after,
    )


def feed_forward(slots, pieces, cot_grad, weight, after=()):
    count, seg_len, width = cot_grad.shape
    share, model = pieces[0].shape[1:]
    outs = call(
        feed_kernel, "feed_forward", MIB, count, 1, (slots,), (*pieces, cot_grad), (weight,),
        [
            shaped((count, seg_len, model), BF), shaped((count, seg_len, width), BF),
            shaped((count, seg_len, 2 * width), BF),
        ] + piece_shapes(count, share, model),
        scratch=[pltpu.VMEM((seg_len, model), F32), pltpu.VMEM((2 * width, model), BF)],
        after=after,
    )
    return outs[0], outs[1], outs[2], outs[3:]


def middle_backward(slots, cot, start, residual, pieces, gain, after=()):
    count, share, model = residual.shape
    return call(
        middle_back_kernel, "middle_backward", MIB, count, count // 2, (slots,),
        (
            (cot, start, True), residual, *pieces[:2], (pieces[2], 0, "early"),
            (pieces[3], 0, "late"),
        ),
        (gain,),
        (shaped((count, share, model), F32), shaped((count, share, model), BF)),
        sums=[shaped((8, model), F32)], after=after,
    )


def first_backward(slots, rows, start, grad, pieces, later, gain, after=()):
    count, share, model = grad.shape
    return call(
        first_back_kernel, "first_backward", MIB, count, count // 2, (slots,),
        (
            (rows, start, True), grad, *[(piece, 0, "early") for piece in pieces],
            *[(piece, 0, "late") for piece in later],
        ),
        (gain,), [shaped((count, share, model), F32)], after=after,
    )[0]


def shared_product(slots, values, weight, after=()):
    count, seg_len, depth = values.shape
    model = weight[0].shape[0] * weight[0].shape[2]
    step = min(2, count)
    return call(
        shared_kernel, "shared_product", MIB, count, step, (slots,), (values,), (weight,),
        piece_shapes(count, seg_len // 4, model),
        scratch=[pltpu.VMEM((step, seg_len, model), F32), pltpu.VMEM((depth, model), BF)],
        after=after,
    )


def cot_backward(cot, start, count, weight, width, after=()):
    seg_len, model = cot.shape[1:]
    return call(
        cot_kernel, "cot_backward", MIB, count, 2, (),
        ((cot, start, False),), (weight,),
        [shaped((count, seg_len, width), F32)], scratch=[pltpu.VMEM((width, model), BF)],
        after=after,
    )[0]


def weight_grad(lefts, rights, extra=None, after=()):
    lefts = [item if isinstance(item, tuple) else (item, 0) for item in lefts]
    model, width = lefts[0][0].shape[2], rights[0].shape[2]
    tile = 2 * LANES
    ins, specs = [], []
    for (left, start), right in zip(lefts, rights):
        ins += [left, right]
        count, depth = right.shape[:2]
        specs += [
            pl.BlockSpec(
                (count, depth, tile), lambda at, block=start // count: (block, 0, at)
            ),
            fixed(right),
        ]
    if extra is not None:
        ins.append(extra)
        specs.append(pl.BlockSpec((tile, LANES), lambda at: (at, 0)))

    def body(*refs):
        weight_grad_kernel(*refs[len(after) :])

    return pl.pallas_call(
        body,
        grid=(model // tile,),
        in_specs=[pl.BlockSpec(memory_space=pl.ANY) for _ in after] + specs,
        out_specs=pl.BlockSpec((tile, width), lambda at: (at, 0)),
        out_shape=shaped((model, width), BF),
        compiler_params=limits(MIB),
        cost_estimate=no_cost(),
        name="weight_grad",
    )(*after, *ins)


def finish_kernel(grad_ref, w_ref, gain_ref, qkv_ref, rest_ref, sum_ref):
    parts, heads = qkv_ref.shape[1:3]
    width = parts * heads * LANES
    values = grad_ref[...].astype(F32)
    for part in range(parts):
        for head in range(heads):
            at = (part * heads + head) * LANES
            qkv_ref[:, part, head, :] = values[:, at : at + LANES]
    rest = values[:, width:]
    rest_ref[...] = rest
    used = lax.broadcasted_iota(jnp.int32, rest.shape, 1) < heads
    weight = w_ref[...].astype(F32)
    total = jnp.sum(weight[:, :width] * values[:, :width], 1, keepdims=True)
    total = total + jnp.sum(jnp.where(used, weight[:, width:] * rest, 0.0), 1, keepdims=True)
    sum_ref[...] = jnp.broadcast_to(total / gain_ref[...], sum_ref.shape)


def finish(grads, weight, gain, heads):
    rows = grads.shape[0]
    outs = [
        shaped((rows, 3, heads, LANES), F32), shaped((rows, LANES), F32), shaped((rows, LANES), F32)
    ]
    ins = (grads, weight, gain)
    return pl.pallas_call(
        finish_kernel,
        grid=(1,),
        in_specs=[fixed(array) for array in ins],
        out_specs=[fixed(out) for out in outs],
        out_shape=outs,
        compiler_params=limits(MIB),
        cost_estimate=no_cost(),
        name="finish",
    )(*ins)


def settle_kernel(gu_ref, down_ref, gu_out, down_out, out_out):
    hidden = gu_out.shape[1]
    half = gu_ref.shape[1] // 2
    flat = gu_ref[...].astype(F32).T
    gu_out[0] = flat[:hidden]
    gu_out[1] = flat[half : half + hidden]
    flat = down_ref[...].astype(F32).T
    down_out[...] = flat[:hidden]
    out_out[...] = flat[half:].reshape(out_out.shape)


def settle(gu_grads, down_out, hidden, heads, after=()):
    rows = gu_grads.shape[0]

    def body(*refs):
        settle_kernel(*refs[len(after) :])

    outs = [
        shaped((2, hidden, rows), F32), shaped((hidden, rows), F32),
        shaped((heads, LANES, rows), F32),
    ]
    return pl.pallas_call(
        body,
        grid=(1,),
        in_specs=[pl.BlockSpec(memory_space=pl.ANY) for _ in after]
        + [fixed(gu_grads), fixed(down_out)],
        out_specs=[fixed(out) for out in outs],
        out_shape=outs,
        compiler_params=limits(MIB),
        cost_estimate=no_cost(),
        name="settle",
    )(*after, gu_grads, down_out)


def fence(values, tokens):
    count = len(values)
    anywhere = pl.BlockSpec(memory_space=pl.ANY)
    return pl.pallas_call(
        lambda *refs: None,
        in_specs=[anywhere] * (count + len(tokens)),
        out_specs=[anywhere] * count,
        out_shape=[shaped(value.shape, value.dtype) for value in values],
        input_output_aliases={at: at for at in range(count)},
        cost_estimate=no_cost(),
        name="fence",
    )(*values, *tokens)


def project_backward(slots, grad, tail, rim, start, count, weights, after=()):
    seg_len = grad.shape[1] - RIM
    model = weights[0].shape[0]
    step = min(2, count)
    return call(
        project_back_kernel, "project_backward", MIB, count, step, (slots,),
        [(array, start, False) for array in (grad, tail, rim)],
        weights, piece_shapes(count, seg_len // 4, model),
        scratch=[
            pltpu.VMEM((step, seg_len, grad.shape[2]), BF), pltpu.VMEM((step, seg_len, model), F32)
        ],
        after=after,
    )


def head_backward(
    ends, first, slots, pieces, out_full, gain, mixed, query, start, heads, after=()
):
    count, model = pieces[0].shape[0], pieces[0].shape[2]
    seg_len, both = query.shape[1:]
    return call(
        lambda ends_ref, first_ref, slots_ref, own, far, core, side, mixed_ref, query_ref,
        out_ref, gain_ref, *outs: head_back_kernel(
            ends_ref, first_ref, slots_ref, own, far, core, side, out_ref, gain_ref, mixed_ref,
            query_ref, *outs
        ),
        "head_backward", MIB, count, min(2, count), (ends, first, slots),
        (*pieces, mixed, (query, start, False)),
        (out_full, gain),
        (
            shaped((count, seg_len, model), BF),
            shaped((count, seg_len, both), BF),
            shaped((count, heads, LANES, LANES), BF),
        ),
        sums=[shaped((8, LANES), F32)], after=after,
    )


def mix_backward(
    ends, first, bias, ext, taps, inverse, grad, state, leave, start, share, after=(), into=()
):
    count, seg_len, both = grad.shape
    wide = ext.shape[2]
    tap_count, width = taps.shape
    return call(
        lambda ends_ref, first_ref, bias_ref, ext_ref, inv_ref, grad_ref, state_ref, leave_ref,
        tap_ref, *rest: mix_back_kernel(
            ends_ref, first_ref, bias_ref, ext_ref, tap_ref, inv_ref, grad_ref, state_ref,
            leave_ref, *rest
        ),
        "mix_backward", MIB, share, BACK_STEP, (ends, first, bias),
        [(array, start, False) for array in (ext, inverse, grad, state, leave)], (taps,),
        (
            shaped((count, seg_len + RIM, wide), BF),
            shaped((count, RIM, width), F32),
            shaped((count, RIM, width), BF),
        ),
        sums=[shaped((8, width), F32), shaped((8, LANES), F32)],
        scratch=[pltpu.VMEM((BACK_STEP, seg_len + 2 * RIM, width), F32)], after=after, first_row=start,
        into=into,
    )


def shifted(value, distance):
    devices = range(lax.axis_size("fsdp"))
    route = [(i - distance, i) for i in devices if i - distance in devices]
    return lax.ppermute(value, "fsdp", route)


def swapped(value, axis, bit):
    return lax.ppermute(value, axis, [(i, i ^ bit) for i in range(lax.axis_size(axis))])


def pick(value, index, axis):
    return lax.dynamic_index_in_dim(value, index, axis, keepdims=False)


def core_sums(pieces, *tokens):
    other_far, other_own, own_far, own = pieces
    got_far = swapped(other_far, "tp", 1)
    got_own = swapped(other_own, "tp", 1)
    got_far = held(got_far, *tokens) if tokens else got_far
    return (own_far.astype(F32) + got_far.astype(F32)).astype(BF), own, got_own


def held(value, *tokens):
    return fence((value,), tokens)[0]


def across(value):
    return swapped(value, "tp", 2)


def beside_core(value):
    return swapped(value, "tp", 1)


def sides():
    return [list(range(at, lax.axis_size("fsdp"), 2)) for at in (0, 1)]


def two_step_gather(own):
    side = lax.axis_index("fsdp") % 2
    mine = lax.all_gather(own, "fsdp", axis=0, axis_index_groups=sides())
    other = swapped(mine, "fsdp", 1)
    return jnp.stack([jnp.where(side == 0, mine, other), jnp.where(side == 0, other, mine)], 1)


def pair_parts(parts, *tokens):
    count = lax.axis_size("fsdp") // 2
    side = lax.axis_index("fsdp") % 2
    view = parts.reshape(count, 2, -1, parts.shape[1])
    return pick(view, side, 1), behind(pick(view, 1 - side, 1), *tokens)


def line_scatter(sums):
    return lax.psum_scatter(
        sums.astype(BF).reshape(-1, sums.shape[-1]), "fsdp", scatter_dimension=0, tiled=True,
        axis_index_groups=sides(),
    )


def doubled_gather(own):
    bit = 1
    index = lax.axis_index("fsdp")
    while bit < lax.axis_size("fsdp"):
        other = swapped(own, "fsdp", bit)
        first = (index & bit) == 0
        own = jnp.concatenate([jnp.where(first, own, other), jnp.where(first, other, own)], 0)
        bit *= 2
    return own


def behind(value, *tokens):
    for token in tokens:
        value = value + (token[(0,) * token.ndim].astype(F32) * 0.0).astype(value.dtype)
    return value


def summed(value, axis):
    bit = 1
    while bit < lax.axis_size(axis):
        value = value + swapped(value, axis, bit)
        bit *= 2
    return value


def apply(maps, states):
    return jnp.einsum("rhij,rhjk->rhik", maps, states, preferred_element_type=F32)


def apply_back(maps, states):
    return jnp.einsum("rhji,rhjk->rhik", maps, states, preferred_element_type=F32)


def halves(value, place):
    count = value.shape[0] // 2
    pair = value.reshape((2, count) + value.shape[1:])
    return pick(pair, place, 0), pick(pair, 1 - place, 0)


def joined(kept, got, place):
    first = jnp.where(place == 0, kept, got)
    second = jnp.where(place == 0, got, kept)
    return jnp.concatenate([first, second], 0)


def relay_forward(decay, local, tokens=()):
    place = lax.axis_index("fsdp") % 2
    turns = lax.axis_size("fsdp") // 2 - 1
    own_decay, send_decay = halves(decay, place)
    own_local, send_local = halves(local, place)
    got_decay, got_local = swapped((send_decay, send_local), "fsdp", 1)
    first_decay = jnp.where(place == 0, own_decay, got_decay)
    first_local = jnp.where(place == 0, own_local, got_local)
    second_decay = jnp.where(place == 0, got_decay, own_decay)
    second_local = jnp.where(place == 0, got_local, own_local)
    pair_decay = apply(second_decay, first_decay).astype(BF)
    pair_local = apply(second_decay, first_local) + second_local.astype(F32)
    state = jnp.zeros_like(own_local)
    for turn in range(turns):
        state = pair_local if turn == 0 else apply(pair_decay, state) + pair_local
        state = behind(state, *tokens[turn]) if turn < len(tokens) else state
        state = shifted(state.astype(BF), 2)
        early_state = state if turn <= max(turns - 2, 0) else early_state
    middle = (apply(first_decay, state) + first_local.astype(F32)).astype(BF)
    got = swapped(jnp.where(place == 0, middle, state), "fsdp", 1)
    entering = joined(jnp.where(place == 0, state, middle), got, place)
    return entering, early_state, (first_decay, second_decay, pair_decay)


def relay_backward(grads, maps, *beside):
    place = lax.axis_index("fsdp") % 2
    turns = lax.axis_size("fsdp") // 2 - 1
    first_decay, second_decay, pair_decay = maps
    beside = list(beside)

    def sent(transfer, value):
        got = transfer(value)
        return held(got, *beside.pop(0)(value)) if beside else got

    own, send = halves(grads, place)
    got = sent(lambda value: swapped(value, "fsdp", 1), send)
    first_grad = jnp.where(place == 0, own, got)
    second_grad = jnp.where(place == 0, got, own)
    pair_grad = apply_back(first_decay, second_grad) + first_grad.astype(F32)
    state = jnp.zeros_like(own)
    for turn in range(turns):
        state = pair_grad if turn == 0 else apply_back(pair_decay, state) + pair_grad
        state = sent(lambda value: shifted(value, -2), state.astype(BF))
    middle = (apply_back(second_decay, state) + second_grad.astype(F32)).astype(BF)
    got = swapped(jnp.where(place == 0, state, middle), "fsdp", 1)
    return joined(jnp.where(place == 0, middle, state), got, place)


def padded(value, lanes):
    return jnp.pad(value, ((0, 0), (0, lanes - value.shape[1])))


def shards(
    layer_input_rows, sequence_lengths, attn_gain, qkv_weight, conv_weight, beta_weight,
    beta_bias, out_gain, out_weight, mlp_gain, gate_up_weight, down_weight, cotangent,
):
    row_count, seg_len, model = layer_input_rows.shape
    chain = lax.axis_size("fsdp")
    place = lax.axis_index("tp")
    segment = lax.axis_index("fsdp")
    tap_count, _, heads, _ = conv_weight.shape
    width = 3 * heads * LANES
    wide = width + LANES
    both = heads * LANES
    hidden_count = down_weight.shape[0]
    hidden_wide = -(-hidden_count // (2 * LANES)) * 2 * LANES
    slice_rows = model // chain
    head_slice = LANES // chain
    first = (segment * seg_len).astype(jnp.int32)
    ends = jnp.cumsum(sequence_lengths, 1).astype(jnp.int32)
    bias = beta_bias.astype(F32)
    near, far = place % 2, place // 2
    slots = jnp.stack(
        [2 * (1 - far) + 1 - near, 2 * far + 1 - near, 2 * (1 - far) + near, 2 * far + near]
    ).astype(jnp.int32)
    first = jnp.stack([first, jnp.int32(0)])

    rim = shifted(layer_input_rows[:, seg_len - RIM :], 1)
    block = padded(beta_weight, LANES)
    flat_qkv = jnp.concatenate([qkv_weight.reshape(slice_rows, width), block], 1)
    cut = flat_qkv.shape[1] * 4 // 7
    more = jnp.concatenate([flat_qkv[:, cut:], out_weight.reshape(both, slice_rows).T], 1)
    weight = lax.all_gather(flat_qkv[:, :cut], "fsdp", axis=0, tiled=True)
    more = two_step_gather(more).reshape(model, -1)
    small = jnp.concatenate([attn_gain, mlp_gain, out_gain, conv_weight.reshape(-1)])
    small = doubled_gather(jnp.pad(small, (0, -small.shape[0] % LANES)).reshape(1, -1))
    attn_scale = small[:, :slice_rows].reshape(1, model).astype(F32)
    mlp_scale = small[:, slice_rows : 2 * slice_rows].reshape(1, model).astype(F32)
    at = 2 * slice_rows
    head_gain = small[:, at : at + head_slice].reshape(1, LANES).astype(F32)
    at += head_slice
    taps = small[:, at : at + tap_count * 3 * heads * head_slice]
    taps = taps.reshape(chain, tap_count, 3 * heads, head_slice).transpose(1, 2, 0, 3)
    taps = taps.reshape(tap_count, width).astype(F32)
    extended = extend(
        layer_input_rows, rim, after=(attn_scale, mlp_scale, head_gain, taps, ends)
    )
    extra = hidden_wide - hidden_count
    weights = (held(weight, extended, more), more)
    gate_up_flip = jnp.pad(gate_up_weight.transpose(1, 2, 0), ((0, 0), (0, extra), (0, 0)))
    feed_weight = jnp.concatenate(
        [
            gate_up_flip.reshape(2 * hidden_wide, slice_rows),
            jnp.pad(down_weight, ((0, extra), (0, 0))),
        ],
        0,
    )

    normed_in, ext, query, local, inverse, decay, state_local = mix_forward(
        ends, first, bias, extended, 0, row_count, attn_scale, weights, taps, heads
    )
    state_in, early_state, maps = relay_forward(decay, state_local)
    feed_weight = lax.all_gather(held(feed_weight, early_state), "fsdp", axis=0)
    gate_up_full, down_full = (feed_weight, 2 * hidden_wide, 0), (feed_weight, hidden_wide, 2)
    mixed, mixed_low, pieces = head_forward(
        ends, first, slots, query, local, state_in, 0, row_count, head_gain, weights[1]
    )
    crossing, kept, near = core_sums(pieces)
    far = across(crossing)
    residual, own = middle_forward(slots, layer_input_rows, 0, (kept, near, far), mlp_scale)
    near, far = beside_core(own), across(own)
    cot_grad = cot_backward(cotangent, 0, row_count, down_full, hidden_wide, after=(own,))
    far = held(far, cot_grad)
    normed_mid, hidden, grad_gate_up, pieces = feed_forward(
        slots, (own, far, near, beside_core(far)), cot_grad, gate_up_full
    )
    half = row_count // 2
    other_far, other_own, own_far, kept = pieces
    got_far, near = beside_core(other_far), beside_core(other_own)
    crossing, rest = (
        (own_far[rows].astype(F32) + got_far[rows].astype(F32)).astype(BF)
        for rows in (slice(0, half), slice(half, row_count))
    )
    grad_gu = weight_grad((normed_mid,), (grad_gate_up,), after=(crossing,))
    far = held(across(crossing), grad_gu)
    gu_grads = lax.psum_scatter(held(grad_gu, far), "fsdp", scatter_dimension=0, tiled=True)
    grad_down = weight_grad(((cotangent, 0),), (hidden,), after=(far,))
    later = held(across(held(rest, far)), grad_down)
    grad_residual, own, mlp_gain_part = middle_backward(
        slots, cotangent, 0, residual, (kept, near, far, later), mlp_scale
    )
    near, far = beside_core(own), across(own)
    output = shared_product(slots, hidden, down_full, after=(own,))
    far = held(far, output[0])
    grad_attn, grad_mixed, grad_state, head_gain_part = head_backward(
        ends, first, slots, (own, far, near, beside_core(far)), weights[1], head_gain, mixed, query,
        0, heads,
    )

    done = []

    def out_beside(value):
        done.append(weight_grad((grad_attn,), (mixed_low,), after=(value,)))
        done.append(jnp.concatenate([grad_down, done[0]], 1))
        return (done[1],)

    def sums_beside(value):
        done.append(core_sums(fence(output, (value,))))
        return (done[2][0],)

    leave = relay_backward(grad_state, maps, out_beside, sums_beside)
    _, down_out, (crossing, kept, near) = done
    far = across(crossing)
    down_out = held(down_out, leave)
    grad_proj, tail, rim_grad, tap_part, bias_part = mix_backward(
        ends, first, bias, ext, taps, inverse, grad_mixed, state_in, leave, 0, row_count,
        after=(down_out,),
    )
    far = held(far, grad_proj)
    layer_output = sum((part.astype(F32) for part in (kept, near, far)), residual).astype(BF)
    down_out = lax.psum_scatter(down_out, "fsdp", scatter_dimension=0, tiled=True)
    rim_back = shifted(rim_grad, -1)

    tap_grad = tap_part[:tap_count].reshape(tap_count * 3 * heads, chain, head_slice)
    tap_grad = tap_grad.transpose(1, 0, 2).reshape(chain, -1)
    small = [
        mlp_gain_part[0].reshape(chain, slice_rows), head_gain_part[0].reshape(chain, head_slice),
        tap_grad,
    ]
    small = jnp.concatenate(small, 1)
    lanes = -(-small.shape[1] // slice_rows)
    small = jnp.pad(small, ((0, 0), (0, lanes * slice_rows - small.shape[1])))
    small = small.reshape(chain, lanes, slice_rows).transpose(0, 2, 1).reshape(model, lanes)
    terms = jnp.stack(split(bias_part[0, :heads]), 1)
    own_lanes = (jnp.arange(chain) == segment).astype(BF)
    terms = (own_lanes[:, None] * terms[:, None, :]).reshape(heads, 2 * chain)
    terms = jnp.pad(terms, ((0, slice_rows - heads), (0, 0)))
    small = jnp.concatenate([small.astype(BF), jnp.tile(terms, (chain, 1))], 1)
    small = jnp.pad(small, ((0, 0), (heads, LANES - heads - small.shape[1])))
    grad_qkv = weight_grad((normed_in,), (grad_proj,), extra=small)
    own_part, sent = pair_parts(grad_qkv, rim_back)
    pieces = project_backward(
        slots, grad_proj, tail, rim_back, 0, half, weights, after=(sent, gu_grads, far)
    )
    crossing, kept, near = core_sums(pieces)
    terms_a = (kept, near, across(crossing))
    pieces = project_backward(
        slots, grad_proj, tail, rim_back, half, half, weights, after=(crossing,)
    )
    got = held(swapped(sent, "fsdp", 1), pieces[0], down_out)
    crossing, kept, near = core_sums(pieces)
    qkv_grads = line_scatter(own_part.astype(F32) + got.astype(F32))
    gate_up_grad, down_grad, out_weight_grad = settle(
        gu_grads, down_out, hidden_count, heads, after=(crossing,)
    )
    terms_b = (kept, near, held(across(crossing), gate_up_grad, layer_output))
    input_grad = first_backward(
        slots, layer_input_rows, 0, grad_residual, terms_a, terms_b, attn_scale,
        after=(gate_up_grad,),
    )
    qkv_grads = held(qkv_grads, gate_up_grad, layer_output)
    qkv_grad, rest_grad, gain_terms = finish(
        qkv_grads, flat_qkv, attn_gain.astype(F32).reshape(slice_rows, 1), heads
    )
    small = rest_grad[:, heads : heads + lanes].T.reshape(-1)
    over_tp = jnp.concatenate([gain_terms[:, 0], small[: slice_rows + head_slice]])
    over_tp = jnp.pad(over_tp, (0, -over_tp.shape[0] % LANES)).reshape(-1, LANES)
    over_tp = summed(over_tp, "tp").reshape(-1)
    at = slice_rows + head_slice
    bias_grad = jnp.sum(
        rest_grad[:heads, heads + lanes : heads + lanes + 2 * chain], 1
    )
    conv_grad = small[at : at + tap_count * 3 * heads * head_slice]
    return (
        layer_output,
        input_grad,
        over_tp[:slice_rows],
        qkv_grad,
        conv_grad.reshape(tap_count, 3, heads, head_slice),
        rest_grad[:, :heads],
        bias_grad,
        over_tp[2 * slice_rows : 2 * slice_rows + head_slice],
        out_weight_grad,
        over_tp[slice_rows : 2 * slice_rows],
        gate_up_grad.transpose(2, 0, 1),
        down_grad,
    )


def solution(mesh):
    in_specs = (
        P(None, "fsdp", None),
        P(),
        P("fsdp"),
        P("fsdp", None, "tp", None),
        P(None, None, "tp", "fsdp"),
        P("fsdp", "tp"),
        P("tp"),
        P("fsdp"),
        P("tp", None, "fsdp"),
        P("fsdp"),
        P("fsdp", None, "tp"),
        P("tp", "fsdp"),
        P(None, "fsdp", None),
    )
    out_specs = (
        P(None, ("fsdp", "tp"), None),
        P(None, ("fsdp", "tp"), None),
        P("fsdp"),
        P("fsdp", None, "tp", None),
        P(None, None, "tp", "fsdp"),
        P("fsdp", "tp"),
        P("tp"),
        P("fsdp"),
        P("tp", None, "fsdp"),
        P("fsdp"),
        P("fsdp", None, "tp"),
        P("tp", "fsdp"),
    )
    return jax.shard_map(shards, mesh=mesh, in_specs=in_specs, out_specs=out_specs, check_vma=False)
```
